32 devices in a mesh: grp: 2 (over y), ep: 16 (over z, x, core), tp: 1.
Axes of the slice: x: 2, y: 2, z: 4, core: 2. Of those that a mesh axis runs over, the one named last changes fastest.
Arguments:
- queries: bfloat16 [2048, 16, 128], P(('grp', 'ep'), 'tp'), parts along dimension 0, may hold values from -8 to 8
- new_keys: bfloat16 [2048, 2, 128], P(('grp', 'ep'), 'tp'), parts along dimension 0, may hold values from -8 to 8
- new_values: bfloat16 [2048, 2, 128], P(('grp', 'ep'), 'tp'), parts along dimension 0, may hold values from -6 to 6
- cache_keys: bfloat16 [2048, 2, 96, 128], P(('grp', 'ep'), 'tp'), parts along dimension 0, may hold values from -8 to 8
- cache_values: bfloat16 [2048, 2, 96, 128], P(('grp', 'ep'), 'tp'), parts along dimension 0, may hold values from -6 to 6
- cache_lengths: int32 [2048], P(('grp', 'ep')), parts along dimension 0, may hold values from 1 to 96, 24576 in all
- residual: bfloat16 [2048, 2048], P(('grp', 'ep')), parts along dimension 0, may hold values from -6 to 6
- out_weight: bfloat16 [2048, 2048], P('tp'), may hold values from -0.125 to 0.125
- norm_gain: float32 [2048], replicated, may hold values from 0.25 to 1.75
- expert_ids: int32 [2048, 8], P(('grp', 'ep')), parts along dimension 0, may hold values from 0 to 15, all different within a row; in each aligned block of 64 rows (0 to 63, 64 to 127, ...) at most 64 rows name the same one
- route_weights: float32 [2048, 8], P(('grp', 'ep')), parts along dimension 0, may hold values from 0.05 to 0.25
- learner_weights: bfloat16 [16, 3, 2048, 768], P(None, None, 'ep', 'tp'), may hold values from -0.125 to 0.125
Outputs:
- hidden_out: bfloat16 [2048, 2048], P(('grp', 'ep'), 'tp'), parts along dimension 0
The draws below stay inside these ranges and needn't reach their ends.
There are 2 independent parts, one for each index of `grp`. The reference program is written for one: setup_inputs(seed, part) draws one part's arguments, and reference() takes and returns one part's arrays. A program takes and returns all parts, laid end to end along the dimension named above; an argument that names none is the same for every part. Nothing has to cross between parts.
Inputs may be any that keep to these rules, and one draw needn't show every extreme that they name: `expert_ids`: each row names 8 different experts. Among the 64 rows of one index of ep no expert is named by more than 64 rows, a bound that some block reaches. `cache_lengths`: the 1024 lengths of one rollout group sum to 24576, and some sequence of each group has all 96 slots live; the whole array, which holds every group laid end to end, sums to that total times the number of groups.
All inputs are finite; a program needn't handle non-finite values.
Results may differ from the reference program's by a relative error of at most 0.0095.
Values may be sent and summed in bfloat16 or wider, within the bound.
No kernel may reach another device: no remote copies, remote signals or barrier semaphores. Data moves between devices by JAX's collectives and lax.ppermute only.
A program may use at most 128 MiB of HBM per device.

```python
import math
import jax
import jax.numpy as jnp
import numpy as np
from jax import lax

D = 2048
FF = 768
QH = 16
KVH = 2
HD = 128
TOP = 8
SEQ_DEV = 64
LEN = 96
EXPERTS = 16
SEQS = 1024
CAP = 64
N_EP = 16
N_TP = 1


def draw_queries(key, part):
    key = jax.random.fold_in(key, 101)
    return jnp.clip(jax.random.normal(key, (SEQS, QH, HD), jnp.float32), -8.0, 8.0).astype(jnp.bfloat16)


def draw_new_keys(key, part):
    key = jax.random.fold_in(key, 102)
    return jnp.clip(jax.random.normal(key, (SEQS, KVH, HD), jnp.float32), -8.0, 8.0).astype(jnp.bfloat16)


def draw_cache_keys(key, part):
    key = jax.random.fold_in(key, 103)
    return jnp.clip(jax.random.normal(key, (SEQS, KVH, LEN, HD), jnp.float32), -8.0, 8.0).astype(jnp.bfloat16)


def level_of(rng, extent, cuts, low, largest):
    def one(axis_at, parts):
        heights = jax.random.uniform(jax.random.fold_in(jax.random.fold_in(rng, 6), axis_at), (parts,), jnp.float32, low / len(cuts), largest / len(cuts))
        return jnp.repeat(jnp.exp(heights), extent[axis_at] // parts).reshape((-1,) + (1,) * (len(extent) - axis_at - 1))

    gain = one(*cuts[0])
    for cut in cuts[1:]:
        gain = gain * one(*cut)
    return gain


def profile(count, total, bound, slope):
    portions = [(1 << 20) // math.isqrt(grade ** slope) + 1 for grade in range(2, count + 1)]
    spare, holding = total - bound - (count - 1), [1] * (count - 1)
    while spare > 0:
        free = [i for i in range(count - 1) if holding[i] < bound]
        pool, budget = sum([portions[i] for i in free]), spare
        for i in free:
            extra = min(bound - holding[i], max(1, budget * portions[i] // pool), spare)
            holding[i] = holding[i] + extra
            spare = spare - extra
    return np.array([bound] + holding)


def uneven_parts(stream_key, count, total, limit, skew):
    if count == 2:
        one = jax.random.randint(stream_key, (), max(1, total - limit), min(limit, total - 1) + 1)
        return jnp.stack([one, total - one])
    lengths = jnp.asarray(profile(count, total, limit, skew), jnp.int32)
    couples = (count - 1) // 2
    giver, sink = lengths[1:1 + 2 * couples:2], lengths[2:2 + 2 * couples:2]
    room = jnp.minimum(giver - 1, limit - sink)
    moved = jax.random.randint(jax.random.fold_in(stream_key, 1), (couples,), 0, 1 << 20) % (room + 1)
    lengths = lengths.at[1:1 + 2 * couples:2].set(giver - moved).at[2:2 + 2 * couples:2].set(sink + moved)
    return lengths[jax.random.permutation(jax.random.fold_in(stream_key, 2), count)]


def assign_block(key, own, number, rows, count, top, bound, lean):
    order = jax.random.permutation(key, count)
    crowded, common = load_shares(count, rows * top, bound, lean, True), load_shares(count, rows * top, bound, lean, False)
    places = jnp.arange(count)

    def named(tallies, rotation):
        used = int((tallies > 0).sum())
        fixed = max(1, used // 4)
        shifted = fixed + (places - fixed + rotation * (used - fixed)) % max(1, count - fixed)
        return jnp.zeros((count,), jnp.int32).at[order[jnp.where(places < fixed, places, shifted)]].set(jnp.asarray(tallies, jnp.int32))

    tallies = jnp.where(number % 4 == 0, named(crowded, number // 4), named(common, number - number // 4 - 1))
    mixed = jax.random.permutation(jax.random.fold_in(own, 3), count)
    giver, sink = mixed[0:count // 2 * 2:2], mixed[1:count // 2 * 2:2]
    room = jnp.minimum(tallies[giver] - 1, bound - tallies[sink]) // 2
    room = jnp.where((giver == order[0]) | (sink == order[0]) | (tallies[sink] == 0), 0, jnp.maximum(room, 0))
    shifted = jax.random.randint(jax.random.fold_in(own, 4), (count // 2,), 0, 1 << 20) % (room + 1)
    tallies = tallies.at[giver].add(-shifted).at[sink].add(shifted)
    labels = jnp.searchsorted(jnp.cumsum(tallies), jnp.arange(rows * top), side="right").astype(jnp.int32)
    table = labels.reshape(top, rows).T
    table = table[jax.random.permutation(jax.random.fold_in(own, 1), rows)]
    rotation = jax.random.randint(jax.random.fold_in(own, 2), (rows, 1), 0, top)
    return jnp.take_along_axis(table, (jnp.arange(top)[None, :] + rotation) % top, axis=1)


def load_shares(count, total, limit, slope, full):
    weights = [(1 << 20) // math.isqrt(rank ** slope) + 1 for rank in range(1, count + 1)]
    largest = limit if full else min(limit, max(-(-total // count), total * weights[0] // sum(weights)))
    least = 1 if total - largest >= count - 1 else 0
    counts, spare = [largest] + [least] * (count - 1), total - largest - least * (count - 1)
    while spare > 0:
        free = [i for i in range(1, count) if counts[i] < largest] or [i for i in range(1, count) if counts[i] < limit]
        mass, left = sum([weights[i] for i in free]), spare
        for i in free:
            addition = min(limit - counts[i], max(1, left * weights[i] // mass), spare)
            counts[i] = counts[i] + addition
            spare = spare - addition
    return np.array(counts)


def noise(own_key, shape, spread, bound, cuts=(), kind=jnp.bfloat16):
    level = level_of(own_key, shape, cuts, -0.22, 0.18) if cuts else 1.0
    drawn = jax.random.normal(own_key, shape, jnp.float32) * spread * level
    return jnp.minimum(jnp.maximum(drawn, -bound), bound).astype(kind)


def setup_inputs(seed: int = 0, part: int = 0) -> dict:
    key_of = jax.random.split(jax.random.key(seed), 13)
    part_splits = jax.random.split(jax.random.fold_in(key_of[12], part), 13)
    queries = draw_queries(jax.random.fold_in(jax.random.fold_in(key_of[12], part), 71), part)
    new_keys = draw_new_keys(jax.random.fold_in(jax.random.fold_in(key_of[12], part), 71), part)
    new_values = noise(part_splits[2], (SEQS, KVH, HD), 1.0, 6.0, ((0, 16),))
    cache_keys = draw_cache_keys(jax.random.fold_in(jax.random.fold_in(key_of[12], part), 71), part)
    cache_values = noise(part_splits[4], (SEQS, KVH, LEN, HD), 1.0, 6.0, ((0, 16),))
    cache_lengths = uneven_parts(part_splits[5], SEQS, SEQS * LEN // 4, LEN, 2).astype(jnp.int32)
    residual = noise(part_splits[6], (SEQS, D), 1.0, 6.0, ((0, 16),))
    out_weight = noise(key_of[7], (QH * HD, D), (QH * HD) ** -0.5, 0.125)
    norm_gain = jnp.clip(1.0 + 0.15 * jax.random.normal(key_of[8], (D,), jnp.float32), 0.25, 1.75)
    expert_ids_keys = jax.random.split(jax.random.fold_in(part_splits[9], 1), SEQS // SEQ_DEV)
    expert_ids_turns = jax.random.permutation(jax.random.fold_in(part_splits[9], 3), SEQS // SEQ_DEV)
    expert_ids = jax.vmap(lambda own, number: assign_block(jax.random.fold_in(part_splits[9], 2), own, number, SEQ_DEV, EXPERTS, TOP, CAP, 2))(expert_ids_keys, expert_ids_turns).reshape((SEQS, TOP))
    route_weights = jnp.clip(0.05 + 0.2 * jax.random.uniform(part_splits[10], (SEQS, TOP), jnp.float32) ** level_of(part_splits[10], (SEQS, TOP), ((0, 16),), -0.2, 0.2), 0.05, 0.25)
    learner_weights = noise(key_of[11], (EXPERTS, 3, D, FF), D ** -0.5, 0.125, ((2, 16),))
    return {"queries": queries, "new_keys": new_keys, "new_values": new_values, "cache_keys": cache_keys, "cache_values": cache_values, "cache_lengths": cache_lengths, "residual": residual, "out_weight": out_weight, "norm_gain": norm_gain, "expert_ids": expert_ids, "route_weights": route_weights, "learner_weights": learner_weights}


def attend(queries, new_keys, new_values, cache_keys, cache_values, cache_lengths):
    seq_count, q_heads, head_size = queries.shape
    kv_heads = cache_keys.shape[1]
    length = cache_keys.shape[2]
    groups = q_heads // kv_heads
    score_scale = head_size ** (-0.5)
    grouped = queries.astype(jnp.float32).reshape(seq_count, kv_heads, groups, head_size)
    scores = jnp.einsum('skgd,skld->skgl', grouped, cache_keys.astype(jnp.float32)) * score_scale
    own_score = jnp.einsum('skgd,skd->skg', grouped, new_keys.astype(jnp.float32)) * score_scale
    live_mask = jnp.arange(length, dtype=jnp.int32)[None, None, None, :] < cache_lengths[:, None, None, None]
    masked = jnp.where(live_mask, scores, -1e+30)
    row_top = jnp.maximum(lax.optimization_barrier(jnp.max(masked, axis=-1)), own_score)
    cache_exp = jnp.where(live_mask, jnp.exp(masked - row_top[..., None]), 0.0)
    own_exp = jnp.exp(own_score - row_top)
    row_total = lax.optimization_barrier(jnp.sum(cache_exp, axis=-1)) + own_exp
    probs_cache = (cache_exp / row_total[..., None]).astype(jnp.bfloat16)
    probs_own = (own_exp / row_total).astype(jnp.bfloat16)
    context = jnp.einsum('skgl,skld->skgd', probs_cache.astype(jnp.float32), cache_values.astype(jnp.float32))
    context = context + probs_own.astype(jnp.float32)[..., None] * new_values.astype(jnp.float32)[:, :, None, :]
    return context.astype(jnp.bfloat16).reshape(seq_count, q_heads * head_size)

def reference(queries, new_keys, new_values, cache_keys, cache_values, cache_lengths, residual, out_weight, norm_gain, expert_ids, route_weights, learner_weights):
    context = attend(queries, new_keys, new_values, cache_keys, cache_values, cache_lengths)
    stream = residual.astype(jnp.float32) + jnp.dot(context, out_weight, preferred_element_type=jnp.float32)
    mean_square = lax.optimization_barrier(jnp.mean(stream * stream, axis=1, keepdims=True))
    normed = (stream * lax.rsqrt(mean_square + 1e-06) * norm_gain).astype(jnp.bfloat16)
    route_total = SEQS * TOP
    slot_total = N_EP * CAP
    block_width = FF // N_TP
    flat_ids = expert_ids.reshape(-1)

    def one_expert(route_store, expert):
        route_hit = flat_ids == expert
        route_index = jnp.nonzero(route_hit, size=slot_total, fill_value=0)[0].astype(jnp.int32)
        live_rows = jnp.arange(slot_total, dtype=jnp.int32) < jnp.sum(route_hit.astype(jnp.int32))
        expert_input = normed[route_index // TOP]
        expert_weights = lax.dynamic_index_in_dim(learner_weights, expert, 0, keepdims=False)
        gate_act = jnp.dot(expert_input, expert_weights[0], preferred_element_type=jnp.float32)
        up_act = jnp.dot(expert_input, expert_weights[1], preferred_element_type=jnp.float32)
        hidden = (jax.nn.silu(gate_act) * up_act).astype(jnp.bfloat16)
        summed = jnp.zeros((slot_total, D), jnp.float32)
        for block in range(N_TP):
            hidden_block = hidden[:, block * block_width:(block + 1) * block_width]
            down_block = expert_weights[2][:, block * block_width:(block + 1) * block_width]
            block_part = lax.dot_general(hidden_block, down_block, (((1,), (1,)), ((), ())), preferred_element_type=jnp.float32)
            summed = summed + lax.optimization_barrier(block_part.astype(jnp.bfloat16)).astype(jnp.float32)
        target = jnp.where(live_rows, route_index, route_total)
        route_store = route_store.at[target].set(summed.astype(jnp.bfloat16), mode='drop')
        return (route_store, None)
    route_store = jnp.zeros((route_total, D), jnp.bfloat16)
    route_store, _ = lax.scan(one_expert, route_store, jnp.arange(EXPERTS, dtype=jnp.int32))
    mixture = jnp.einsum('std,st->sd', route_store.reshape(SEQS, TOP, D).astype(jnp.float32), route_weights, precision=lax.Precision.HIGHEST)
    return (stream + mixture).astype(jnp.bfloat16)
```

```python
import functools

import jax
import jax.numpy as jnp
from jax import lax
from jax.experimental import pallas as pl
from jax.experimental.pallas import tpu as pltpu
from jax.sharding import PartitionSpec as P

LANES = 128


def attend(queries, new_keys, new_values, cache_keys, cache_values, cache_lengths):
    seq_count, q_heads, head_size = queries.shape
    kv_heads = cache_keys.shape[1]
    length = cache_keys.shape[2]
    groups = q_heads // kv_heads
    score_scale = head_size ** (-0.5)
    grouped = queries.reshape(seq_count, kv_heads, groups, head_size)
    scores = (
        jnp.einsum("skgd,skld->skgl", grouped, cache_keys, preferred_element_type=jnp.float32)
        * score_scale
    )
    own_score = (
        jnp.einsum("skgd,skd->skg", grouped, new_keys, preferred_element_type=jnp.float32)
        * score_scale
    )
    live_mask = (
        jnp.arange(length, dtype=jnp.int32)[None, None, None, :]
        < cache_lengths[:, None, None, None]
    )
    masked = jnp.where(live_mask, scores, -1e30)
    row_top = jnp.maximum(jnp.max(masked, axis=-1), own_score)
    cache_exp = jnp.where(live_mask, jnp.exp(masked - row_top[..., None]), 0.0)
    own_exp = jnp.exp(own_score - row_top)
    row_total = jnp.sum(cache_exp, axis=-1) + own_exp
    probs_cache = (cache_exp / row_total[..., None]).astype(jnp.bfloat16)
    probs_own = (own_exp / row_total).astype(jnp.bfloat16)
    context = jnp.einsum(
        "skgl,skld->skgd", probs_cache, cache_values, preferred_element_type=jnp.float32
    )
    context = (
        context
        + probs_own.astype(jnp.float32)[..., None] * new_values.astype(jnp.float32)[:, :, None, :]
    )
    return context.astype(jnp.bfloat16).reshape(seq_count, q_heads * head_size)


def swap_ep(x, bits):
    count = lax.axis_size("ep")
    return lax.ppermute(x, "ep", [(i, i ^ bits) for i in range(count)])


def swap_grp(x):
    return lax.ppermute(x, "grp", [(0, 1), (1, 0)])


def gather_weights(learner_weights, shared):
    ff = learner_weights.shape[3]
    count = lax.axis_size("ep")
    me = lax.axis_index("ep")
    grp = lax.axis_index("grp")
    rows = learner_weights.shape[2]
    half = ff // 2
    pieces = []
    for bits in range(count - 1, -1, -1):
        if bits in shared:
            block = lax.dynamic_slice(
                learner_weights, (me ^ bits, 0, 0, grp * half), (1, 3, rows, half)
            )[0]
            mine = swap_ep(block, bits)
            pieces.append((bits, 0, mine))
            pieces.append((bits, 1, swap_grp(mine)))
        else:
            block = lax.dynamic_index_in_dim(learner_weights, me ^ bits, 0, keepdims=False)
            pieces.append((bits, None, swap_ep(block, bits) if bits else block))
    return pieces


def expert_kernel(places, width, experts, where_ref, x_ref, *refs):
    piece_refs = refs[: len(places)]
    out_ref, weights, sems = refs[len(places) :]
    me, grp = where_ref[0], where_ref[1]
    rows, ff = piece_refs[0].shape[1], weights.shape[2]
    half = ff // 2

    @pl.when(pl.program_id(0) == 0)
    def load():
        copies = []
        for index, (bits, part) in enumerate(places):
            row = pl.ds(pl.multiple_of((me ^ bits) * rows, rows), rows)
            if part is None:
                target = weights.at[:, row, :]
            else:
                start = pl.multiple_of((grp ^ part) * half, LANES)
                target = weights.at[:, row, pl.ds(start, half)]
            copies.append(pltpu.make_async_copy(piece_refs[index], target, sems.at[index]))
        for copy in copies:
            copy.start()
        for copy in copies:
            copy.wait()

    x = x_ref[:, :width]
    extra = x_ref[:, width:].astype(jnp.float32)
    lane = lax.broadcasted_iota(jnp.int32, extra.shape, 1)
    picked = jnp.where((lane == me) | (lane == me + experts), extra, 0.0)
    coef = jnp.sum(picked, axis=1, keepdims=True)
    gate = jnp.dot(x, weights[0], preferred_element_type=jnp.float32)
    up = jnp.dot(x, weights[1], preferred_element_type=jnp.float32)
    hidden = (gate / (1.0 + jnp.exp(-gate)) * up).astype(jnp.bfloat16)
    down = lax.dot_general(
        hidden, weights[2], (((1,), (1,)), ((), ())), preferred_element_type=jnp.float32
    )
    out_ref[...] = (down * coef).astype(jnp.bfloat16)


def run_expert(tokens, pieces, width, experts):
    total, ext = tokens.shape
    ff = max(p[2].shape[2] for p in pieces)
    tile = 256 if total % 256 == 0 else total
    where = jnp.stack([lax.axis_index("ep"), lax.axis_index("grp")]).astype(jnp.int32)
    places = [(p[0], p[1]) for p in pieces]
    grid_spec = pltpu.PrefetchScalarGridSpec(
        num_scalar_prefetch=1,
        grid=(total // tile,),
        in_specs=[pl.BlockSpec((tile, ext), lambda i, w: (i, 0))]
        + [pl.BlockSpec(memory_space=pl.ANY)] * len(pieces),
        out_specs=pl.BlockSpec((tile, width), lambda i, w: (i, 0)),
        scratch_shapes=[
            pltpu.VMEM((3, width, ff), jnp.bfloat16),
            pltpu.SemaphoreType.DMA((len(pieces),)),
        ],
    )
    return pl.pallas_call(
        functools.partial(expert_kernel, places, width, experts),
        grid_spec=grid_spec,
        out_shape=jax.ShapeDtypeStruct((total, width), jnp.bfloat16),
        compiler_params=pltpu.CompilerParams(vmem_limit_bytes=40 * 1024 * 1024),
    )(where, tokens, *[p[2] for p in pieces])


def shards(
    queries,
    new_keys,
    new_values,
    cache_keys,
    cache_values,
    cache_lengths,
    residual,
    out_weight,
    norm_gain,
    expert_ids,
    route_weights,
    learner_weights,
):
    seq_count, width = residual.shape
    experts = learner_weights.shape[0]
    ff = learner_weights.shape[3]
    count = lax.axis_size("ep")
    parts = lax.axis_size("tp")
    stages = [1 << b for b in range(count.bit_length() - 2, -1, -1)]

    split = ff % (2 * LANES) == 0 and lax.axis_size("grp") == 2
    shared = set(range(count // 4, count)) if split else set()
    pieces = gather_weights(learner_weights, shared)

    context = attend(queries, new_keys, new_values, cache_keys, cache_values, cache_lengths)
    attn = jnp.dot(context, out_weight, preferred_element_type=jnp.float32)
    if parts > 1:
        attn = lax.psum(attn, "tp")
    stream = residual.astype(jnp.float32) + attn
    mean_square = jnp.mean(stream * stream, axis=1, keepdims=True)
    normed = (stream * lax.rsqrt(mean_square + 1e-06) * norm_gain).astype(jnp.bfloat16)

    hit = expert_ids[:, :, None] == jnp.arange(experts, dtype=jnp.int32)[None, None, :]
    coefs = jnp.sum(jnp.where(hit, route_weights[:, :, None], 0.0), axis=1)
    coarse = coefs.astype(jnp.bfloat16)
    fine = (coefs - coarse.astype(jnp.float32)).astype(jnp.bfloat16)
    tail = -(2 * experts) % LANES
    tokens = jnp.concatenate(
        [normed, coarse, fine, jnp.zeros((seq_count, tail), jnp.bfloat16)], axis=1
    )
    for bits in stages:
        tokens = jnp.concatenate([tokens, swap_ep(tokens, bits)], axis=0)

    terms = run_expert(tokens, pieces, width, experts)
    for bits in reversed(stages):
        keep = terms.shape[0] // 2
        other = swap_ep(terms[keep:], bits)
        terms = terms[:keep].astype(jnp.float32) + other.astype(jnp.float32)
        if bits != stages[0]:
            terms = terms.astype(jnp.bfloat16)
    if parts > 1:
        terms = lax.psum_scatter(terms, "tp", scatter_dimension=1, tiled=True)
        own = width // parts
        stream = lax.dynamic_slice_in_dim(stream, lax.axis_index("tp") * own, own, 1)
    return (stream + terms).astype(jnp.bfloat16)


def solution(mesh):
    return jax.shard_map(
        shards,
        mesh=mesh,
        in_specs=(
            P(("grp", "ep"), "tp", None),
            P(("grp", "ep"), "tp", None),
            P(("grp", "ep"), "tp", None),
            P(("grp", "ep"), "tp", None, None),
            P(("grp", "ep"), "tp", None, None),
            P(("grp", "ep")),
            P(("grp", "ep"), None),
            P("tp", None),
            P(),
            P(("grp", "ep"), None),
            P(("grp", "ep"), None),
            P(None, None, "ep", "tp"),
        ),
        out_specs=P(("grp", "ep"), "tp"),
        check_vma=False,
    )
```

```python
import functools

import jax
import jax.numpy as jnp
from jax import lax
from jax.experimental import pallas as pl
from jax.experimental.pallas import tpu as pltpu
from jax.sharding import PartitionSpec as P

LANES = 128


def attend(queries, new_keys, new_values, cache_keys, cache_values, cache_lengths):
    seq_count, q_heads, head_size = queries.shape
    kv_heads = cache_keys.shape[1]
    length = cache_keys.shape[2]
    groups = q_heads // kv_heads
    score_scale = head_size ** (-0.5)
    grouped = queries.reshape(seq_count, kv_heads, groups, head_size)
    scores = (
        jnp.einsum("skgd,skld->skgl", grouped, cache_keys, preferred_element_type=jnp.float32)
        * score_scale
    )
    own_score = (
        jnp.einsum("skgd,skd->skg", grouped, new_keys, preferred_element_type=jnp.float32)
        * score_scale
    )
    live_mask = (
        jnp.arange(length, dtype=jnp.int32)[None, None, None, :]
        < cache_lengths[:, None, None, None]
    )
    masked = jnp.where(live_mask, scores, -1e30)
    row_top = jnp.maximum(jnp.max(masked, axis=-1), own_score)
    cache_exp = jnp.where(live_mask, jnp.exp(masked - row_top[..., None]), 0.0)
    own_exp = jnp.exp(own_score - row_top)
    row_total = jnp.sum(cache_exp, axis=-1) + own_exp
    probs_cache = (cache_exp / row_total[..., None]).astype(jnp.bfloat16)
    probs_own = (own_exp / row_total).astype(jnp.bfloat16)
    context = jnp.einsum(
        "skgl,skld->skgd", probs_cache, cache_values, preferred_element_type=jnp.float32
    )
    context = (
        context
        + probs_own.astype(jnp.float32)[..., None] * new_values.astype(jnp.float32)[:, :, None, :]
    )
    return context.astype(jnp.bfloat16).reshape(seq_count, q_heads * head_size)


def swap_ep(x, bits):
    count = lax.axis_size("ep")
    return lax.ppermute(x, "ep", [(i, i ^ bits) for i in range(count)])


def swap_grp(x):
    return lax.ppermute(x, "grp", [(0, 1), (1, 0)])


def after(values, others):
    if not others:
        return values
    return lax.optimization_barrier((tuple(values), tuple(others)))[0]


def load_weights(places, piece_refs, weights, sems, grp):
    half = weights.shape[-1] // 2
    copies = []
    for index, (lead, part) in enumerate(places):
        tail = (slice(None),) * (len(weights.shape) - 1 - len(lead))
        if part is None:
            target = weights.at[lead + tail]
        else:
            start = pl.multiple_of((grp ^ part) * half, LANES)
            target = weights.at[lead + tail + (pl.ds(start, half),)]
        copies.append(pltpu.make_async_copy(piece_refs[index], target, sems.at[index]))
    for copy in copies:
        copy.start()
    for copy in copies:
        copy.wait()


def hidden_kernel(places, where_ref, x_ref, *refs):
    piece_refs = refs[: len(places)]
    out_ref, weights, sems = refs[len(places) :]

    @pl.when(pl.program_id(0) == 0)
    def load():
        load_weights(places, piece_refs, weights, sems, where_ref[1])

    x = x_ref[...]
    gate = jnp.dot(x, weights[0], preferred_element_type=jnp.float32)
    up = jnp.dot(x, weights[1], preferred_element_type=jnp.float32)
    out_ref[...] = (gate / (1.0 + jnp.exp(-gate)) * up).astype(jnp.bfloat16)


def down_kernel(places, experts, where_ref, hidden_ref, extra_ref, *refs):
    piece_refs = refs[: len(places)]
    out_refs, (weights, sems) = refs[len(places) : -2], refs[-2:]
    me = where_ref[0]

    @pl.when(pl.program_id(0) == 0)
    def load():
        load_weights(places, piece_refs, weights, sems, where_ref[1])

    extra = extra_ref[...].astype(jnp.float32)
    lane = lax.broadcasted_iota(jnp.int32, extra.shape, 1)
    picked = jnp.where((lane == me) | (lane == me + experts), extra, 0.0)
    coef = jnp.sum(picked, axis=1, keepdims=True)
    matrix = weights[...]
    down = lax.dot_general(
        hidden_ref[...],
        matrix.reshape(-1, matrix.shape[-1]),
        (((1,), (1,)), ((), ())),
        preferred_element_type=jnp.float32,
    )
    down = (down * coef).astype(jnp.bfloat16)
    start = 0
    for out_ref in out_refs:
        out_ref[...] = down[:, start : start + out_ref.shape[1]]
        start += out_ref.shape[1]


def call_local(kernel, grid, in_specs, out_specs, out_shape, scratch, operands, pieces):
    where = jnp.stack([lax.axis_index("ep"), lax.axis_index("grp")]).astype(jnp.int32)
    grid_spec = pltpu.PrefetchScalarGridSpec(
        num_scalar_prefetch=1,
        grid=grid,
        in_specs=in_specs + [pl.BlockSpec(memory_space=pl.ANY)] * len(pieces),
        out_specs=out_specs,
        scratch_shapes=[
            pltpu.VMEM(scratch, jnp.bfloat16),
            pltpu.SemaphoreType.DMA((len(pieces),)),
        ],
    )
    return pl.pallas_call(
        kernel,
        grid_spec=grid_spec,
        out_shape=out_shape,
        compiler_params=pltpu.CompilerParams(vmem_limit_bytes=56 * 1024 * 1024),
    )(where, *operands, *[array for _, _, array in pieces])


def run_hidden(tokens, pieces, width, ff):
    total = tokens.shape[0]
    tile = 256 if total % 256 == 0 else total
    return call_local(
        functools.partial(hidden_kernel, [p[:2] for p in pieces]),
        (total // tile,),
        [pl.BlockSpec((tile, width), lambda i, w: (i, 0))],
        pl.BlockSpec((tile, ff), lambda i, w: (i, 0)),
        jax.ShapeDtypeStruct((total, ff), jnp.bfloat16),
        (2, width, ff),
        [tokens],
        pieces,
    )


def run_down(hidden, tokens, pieces, shape, columns, experts):
    total, ff = hidden.shape
    tile = 256 if total % 256 == 0 else total
    width = sum(columns)
    extra = tokens.shape[1] - width
    return call_local(
        functools.partial(down_kernel, [p[:2] for p in pieces], experts),
        (total // tile,),
        [
            pl.BlockSpec((tile, ff), lambda i, w: (i, 0)),
            pl.BlockSpec((tile, extra), lambda i, w: (i, width // extra)),
        ],
        [pl.BlockSpec((tile, c), lambda i, w: (i, 0)) for c in columns],
        [jax.ShapeDtypeStruct((total, c), jnp.bfloat16) for c in columns],
        shape,
        [hidden, tokens],
        pieces,
    )


def fold(terms, axis, bits):
    keep = lax.index_in_dim(terms, 0, axis, keepdims=False)
    give = lax.index_in_dim(terms, 1, axis, keepdims=False)
    other = swap_ep(give, bits)
    return (keep.astype(jnp.float32) + other.astype(jnp.float32)).astype(jnp.bfloat16)


def reduce_blocks(terms, stages, order, seq_count):
    left = list(reversed(stages))
    terms = terms.reshape((2,) * len(left) + (seq_count, terms.shape[1]))
    for bits in order:
        axis = left.index(bits)
        left.pop(axis)
        terms = fold(terms, axis, bits)
    return terms


def shards(
    queries,
    new_keys,
    new_values,
    cache_keys,
    cache_values,
    cache_lengths,
    residual,
    out_weight,
    norm_gain,
    expert_ids,
    route_weights,
    learner_weights,
):
    seq_count, width = residual.shape
    experts, _, rows, ff = learner_weights.shape
    count = lax.axis_size("ep")
    parts = lax.axis_size("tp")
    grp = lax.axis_index("grp")
    stages = [1 << b for b in range(count.bit_length() - 2, -1, -1)]
    split = ff % (2 * LANES) == 0 and lax.axis_size("grp") == 2
    half = ff // 2

    def bring(matrix, low, high, halved, deps):
        start, size = (grp * half, half) if halved else (0, ff)
        block = lax.dynamic_slice(
            learner_weights, (0, matrix, low, start), (experts, 1, high - low, size)
        )[:, 0]
        (block,) = after([block], deps)
        return lax.all_to_all(block, "ep", split_axis=0, concat_axis=0, tiled=True)

    def both(lead, mine):
        if not split:
            return [(lead, None, mine)]
        return [(lead, 0, mine), (lead, 1, swap_grp(mine))]

    def arrays(pieces):
        return [array for _, _, array in pieces]

    cut = rows * 3 // 4 // 16 * 16
    size = half if split else ff
    gate = bring(0, 0, rows, split, [])

    context = attend(queries, new_keys, new_values, cache_keys, cache_values, cache_lengths)
    attn = jnp.dot(context, out_weight, preferred_element_type=jnp.float32)
    if parts > 1:
        attn = lax.psum(attn, "tp")
    stream = residual.astype(jnp.float32) + attn
    mean_square = jnp.mean(stream * stream, axis=1, keepdims=True)
    normed = (stream * lax.rsqrt(mean_square + 1e-06) * norm_gain).astype(jnp.bfloat16)

    hit = expert_ids[:, :, None] == jnp.arange(experts, dtype=jnp.int32)[None, None, :]
    coefs = jnp.sum(jnp.where(hit, route_weights[:, :, None], 0.0), axis=1)
    coarse = coefs.astype(jnp.bfloat16)
    fine = (coefs - coarse.astype(jnp.float32)).astype(jnp.bfloat16)
    pad = -(2 * experts) % LANES
    tokens = jnp.concatenate(
        [normed, coarse, fine, jnp.zeros((seq_count, pad), jnp.bfloat16)], axis=1
    )

    def gather(tokens, bits):
        return jnp.concatenate([tokens, swap_ep(tokens, bits)], axis=0)

    def gathers(tokens, todo):
        for bits in todo:
            tokens = gather(tokens, bits)
        return tokens

    rest = len(stages) - 3
    tokens = gathers(tokens, stages[:rest])
    up = bring(1, 0, rows, split, [gate, tokens])
    gate = both((0,), gate.reshape(width, size))
    tokens = gathers(tokens, stages[rest : rest + 1])
    down_a = bring(2, 0, cut, split, [up, tokens] + arrays(gate))
    up = both((1,), up.reshape(width, size))
    tokens = gathers(tokens, stages[rest + 1 : rest + 2])
    down_b = bring(2, cut, rows, False, [down_a, tokens] + arrays(up))
    down_a = both((slice(None), pl.ds(0, cut)), down_a)
    tokens = gathers(tokens, stages[rest + 2 :])

    hidden = run_hidden(tokens, gate + up, width, ff)
    near_first = stages[::-1]
    far_first = [1] + stages[-3::-1] + [2] if len(stages) > 2 else near_first
    pieces = down_a + [((slice(None), pl.ds(cut, rows - cut)), None, down_b)]
    columns = [width // 2, width - width // 2]
    terms = run_down(hidden, tokens, pieces, (count, rows, ff), columns, experts)
    totals = [
        reduce_blocks(term, stages, order, seq_count)
        for term, order in zip(terms, (near_first, far_first))
    ]
    terms = jnp.concatenate(totals, axis=1).astype(jnp.float32)
    if parts > 1:
        terms = lax.psum_scatter(terms, "tp", scatter_dimension=1, tiled=True)
        own = width // parts
        stream = lax.dynamic_slice_in_dim(stream, lax.axis_index("tp") * own, own, 1)
    return (stream + terms).astype(jnp.bfloat16)


def solution(mesh):
    return jax.shard_map(
        shards,
        mesh=mesh,
        in_specs=(
            P(("grp", "ep"), "tp", None),
            P(("grp", "ep"), "tp", None),
            P(("grp", "ep"), "tp", None),
            P(("grp", "ep"), "tp", None, None),
            P(("grp", "ep"), "tp", None, None),
            P(("grp", "ep")),
            P(("grp", "ep"), None),
            P("tp", None),
            P(),
            P(("grp", "ep"), None),
            P(("grp", "ep"), None),
            P(None, None, "ep", "tp"),
        ),
        out_specs=P(("grp", "ep"), "tp"),
        check_vma=False,
    )
```

```python
import functools

import jax
import jax.numpy as jnp
from jax import lax
from jax.experimental import pallas as pl
from jax.experimental.pallas import tpu as pltpu
from jax.sharding import PartitionSpec as P

LANES = 128


def attend(queries, new_keys, new_values, cache_keys, cache_values, cache_lengths):
    seq_count, q_heads, head_size = queries.shape
    kv_heads = cache_keys.shape[1]
    length = cache_keys.shape[2]
    groups = q_heads // kv_heads
    score_scale = head_size ** (-0.5)
    grouped = queries.reshape(seq_count, kv_heads, groups, head_size)
    scores = (
        jnp.einsum("skgd,skld->skgl", grouped, cache_keys, preferred_element_type=jnp.float32)
        * score_scale
    )
    own_score = (
        jnp.einsum("skgd,skd->skg", grouped, new_keys, preferred_element_type=jnp.float32)
        * score_scale
    )
    live_mask = (
        jnp.arange(length, dtype=jnp.int32)[None, None, None, :]
        < cache_lengths[:, None, None, None]
    )
    masked = jnp.where(live_mask, scores, -1e30)
    row_top = jnp.maximum(jnp.max(masked, axis=-1), own_score)
    cache_exp = jnp.where(live_mask, jnp.exp(masked - row_top[..., None]), 0.0)
    own_exp = jnp.exp(own_score - row_top)
    row_total = jnp.sum(cache_exp, axis=-1) + own_exp
    probs_cache = (cache_exp / row_total[..., None]).astype(jnp.bfloat16)
    probs_own = (own_exp / row_total).astype(jnp.bfloat16)
    context = jnp.einsum(
        "skgl,skld->skgd", probs_cache, cache_values, preferred_element_type=jnp.float32
    )
    context = (
        context
        + probs_own.astype(jnp.float32)[..., None] * new_values.astype(jnp.float32)[:, :, None, :]
    )
    return context.astype(jnp.bfloat16).reshape(seq_count, q_heads * head_size)


def swap_ep(x, bits):
    count = lax.axis_size("ep")
    return lax.ppermute(x, "ep", [(i, i ^ bits) for i in range(count)])


def swap_grp(x):
    return lax.ppermute(x, "grp", [(0, 1), (1, 0)])


def after(values, others):
    if not others:
        return values
    return lax.optimization_barrier((tuple(values), tuple(others)))[0]


def load_weights(places, piece_refs, weights, sems, grp):
    half = weights.shape[-1] // 2
    copies = []
    for index, (source, lead, part) in enumerate(places):
        piece = piece_refs[index]
        if source is not None:
            piece = piece.at[source]
        tail = (slice(None),) * (len(weights.shape) - 1 - len(lead))
        if part is None:
            target = weights.at[lead + tail]
        else:
            start = pl.multiple_of((grp ^ part) * half, LANES)
            target = weights.at[lead + tail + (pl.ds(start, half),)]
        copies.append(pltpu.make_async_copy(piece, target, sems.at[index]))
    for copy in copies:
        copy.start()
    for copy in copies:
        copy.wait()


def hidden_kernel(places, experts, where_ref, x_ref, *refs):
    piece_refs = refs[: len(places)]
    out_ref, weights, sems = refs[len(places) :]
    me = where_ref[0]

    @pl.when(pl.program_id(0) == 0)
    def load():
        load_weights(places, piece_refs, weights, sems, where_ref[1])

    width = weights.shape[1]
    extra = x_ref[:, width:].astype(jnp.float32)
    lane = lax.broadcasted_iota(jnp.int32, extra.shape, 1)
    picked = jnp.where((lane == me) | (lane == me + experts), extra, 0.0)
    coef = jnp.sum(picked, axis=1, keepdims=True)
    x = x_ref[:, :width]
    gate = jnp.dot(x, weights[0], preferred_element_type=jnp.float32)
    up = jnp.dot(x, weights[1], preferred_element_type=jnp.float32)
    out_ref[...] = (gate / (1.0 + jnp.exp(-gate)) * up * coef).astype(jnp.bfloat16)


def down_kernel(places, where_ref, hidden_ref, *refs):
    piece_refs = refs[: len(places)]
    out_refs, weights = refs[len(places) : -1], refs[-1]
    grp = where_ref[1]
    step = pl.program_id(0)
    half = weights.shape[-1] // 2
    for ref, (low, part) in zip(piece_refs, places):
        span = slice(low, low + ref.shape[1])
        if part is None:
            weights[:, span, :] = ref[...]
        else:
            start = pl.multiple_of((grp ^ part) * half, LANES)
            weights[:, span, pl.ds(start, half)] = ref[...]
    matrix = weights[...]
    down = lax.dot_general(
        hidden_ref[...],
        matrix.reshape(-1, matrix.shape[-1]),
        (((1,), (1,)), ((), ())),
        preferred_element_type=jnp.float32,
    )
    down = down.astype(jnp.bfloat16)
    size = out_refs[0].shape[0]
    turn = pl.num_programs(0) // 2
    for column in range(2):

        @pl.when((step >= turn) == (column == 1))
        def store(column=column):
            out_refs[2 * column][...] = down[:size]
            out_refs[2 * column + 1][...] = down[size:]


def call_local(kernel, grid, in_specs, out_specs, out_shape, scratch, operands, pieces):
    where = jnp.stack([lax.axis_index("ep"), lax.axis_index("grp")]).astype(jnp.int32)
    grid_spec = pltpu.PrefetchScalarGridSpec(
        num_scalar_prefetch=1,
        grid=grid,
        in_specs=in_specs + [pl.BlockSpec(memory_space=pl.ANY)] * len(pieces),
        out_specs=out_specs,
        scratch_shapes=[
            pltpu.VMEM(scratch, jnp.bfloat16),
            pltpu.SemaphoreType.DMA((len(pieces),)),
        ],
    )
    return pl.pallas_call(
        kernel,
        grid_spec=grid_spec,
        out_shape=out_shape,
        compiler_params=pltpu.CompilerParams(vmem_limit_bytes=56 * 1024 * 1024),
    )(where, *operands, *[piece[3] for piece in pieces])


def run_hidden(tokens, pieces, width, ff, experts):
    total = tokens.shape[0]
    tile = 256 if total % 256 == 0 else total
    return call_local(
        functools.partial(hidden_kernel, [p[:3] for p in pieces], experts),
        (total // tile,),
        [pl.BlockSpec((tile, tokens.shape[1]), lambda i, w: (i, 0))],
        pl.BlockSpec((tile, ff), lambda i, w: (i, 0)),
        jax.ShapeDtypeStruct((total, ff), jnp.bfloat16),
        (2, width, ff),
        [tokens],
        pieces,
    )


def run_down(hidden, pieces, count, rows, width):
    total, ff = hidden.shape
    block = min(max(4, 4 * LANES // rows), count // 2)
    steps = count // block
    where = jnp.stack([lax.axis_index("ep"), lax.axis_index("grp")]).astype(jnp.int32)
    spec = (total // 2, block * rows)
    low = pl.BlockSpec(spec, lambda i, w: (0, jnp.minimum(i, steps // 2 - 1)))
    high = pl.BlockSpec(spec, lambda i, w: (0, jnp.maximum(i - steps // 2, 0)))
    grid_spec = pltpu.PrefetchScalarGridSpec(
        num_scalar_prefetch=1,
        grid=(steps,),
        in_specs=[pl.BlockSpec((total, ff), lambda i, w: (0, 0))]
        + [pl.BlockSpec((block,) + p[3].shape[1:], lambda i, w: (i, 0, 0)) for p in pieces],
        out_specs=[low, low, high, high],
        scratch_shapes=[pltpu.VMEM((block, rows, ff), jnp.bfloat16)],
    )
    return pl.pallas_call(
        functools.partial(down_kernel, [p[1:3] for p in pieces]),
        grid_spec=grid_spec,
        out_shape=[jax.ShapeDtypeStruct((total // 2, width // 2), jnp.bfloat16)] * 4,
        compiler_params=pltpu.CompilerParams(vmem_limit_bytes=56 * 1024 * 1024),
    )(where, hidden, *[piece[3] for piece in pieces])


def add_terms(mine, other):
    return (mine.astype(jnp.float32) + other.astype(jnp.float32)).astype(jnp.bfloat16)


def fold(terms, axis, bits):
    keep = lax.index_in_dim(terms, 0, axis, keepdims=False)
    give = lax.index_in_dim(terms, 1, axis, keepdims=False)
    return add_terms(keep, swap_ep(give, bits))


def reduce_blocks(terms, left, order, seq_count):
    left = list(left)
    terms = terms.reshape((2,) * len(left) + (seq_count, terms.shape[1]))
    for bits in order:
        axis = left.index(bits)
        left.pop(axis)
        terms = fold(terms, axis, bits)
    return terms


def shards(
    queries,
    new_keys,
    new_values,
    cache_keys,
    cache_values,
    cache_lengths,
    residual,
    out_weight,
    norm_gain,
    expert_ids,
    route_weights,
    learner_weights,
):
    seq_count, width = residual.shape
    experts, _, rows, ff = learner_weights.shape
    count = lax.axis_size("ep")
    parts = lax.axis_size("tp")
    grp = lax.axis_index("grp")
    stages = [1 << b for b in range(count.bit_length() - 2, -1, -1)]
    split = ff % (2 * LANES) == 0 and lax.axis_size("grp") == 2
    half = ff // 2

    def cut_out(matrix, low, high, halved, start):
        start, size = (start, half) if halved else (0, ff)
        return lax.dynamic_slice(
            learner_weights, (0, matrix, low, start), (experts, 1, high - low, size)
        )[:, 0]

    def bring(block, deps):
        (block,) = after([block], deps)
        return lax.all_to_all(block, "ep", split_axis=0, concat_axis=0, tiled=True)

    def both(lead, mine):
        if not split:
            return [(None, lead, None, mine)]
        return [(None, lead, 0, mine), (None, lead, 1, swap_grp(mine))]

    def arrays(pieces):
        return [piece[3] for piece in pieces]

    cut = rows * 3 // 4 // 16 * 16
    size = half if split else ff
    gate_block = cut_out(0, 0, rows, split, grp * half)
    (start,) = after([grp * half], [gate_block])
    up_block = cut_out(1, 0, rows, split, start)
    down_a_block = cut_out(2, 0, cut, split, start)
    down_b_block = cut_out(2, cut, rows, False, start)
    gate = bring(gate_block, [])
    (gate,) = after([gate], [up_block, down_a_block, down_b_block])

    context = attend(queries, new_keys, new_values, cache_keys, cache_values, cache_lengths)
    attn = jnp.dot(context, out_weight, preferred_element_type=jnp.float32)
    if parts > 1:
        attn = lax.psum(attn, "tp")
    stream = residual.astype(jnp.float32) + attn
    mean_square = jnp.mean(stream * stream, axis=1, keepdims=True)
    normed = (stream * lax.rsqrt(mean_square + 1e-06) * norm_gain).astype(jnp.bfloat16)

    hit = expert_ids[:, :, None] == jnp.arange(experts, dtype=jnp.int32)[None, None, :]
    coefs = jnp.sum(jnp.where(hit, route_weights[:, :, None], 0.0), axis=1)
    coarse = coefs.astype(jnp.bfloat16)
    fine = (coefs - coarse.astype(jnp.float32)).astype(jnp.bfloat16)
    pad = -(2 * experts) % LANES
    tokens = jnp.concatenate(
        [normed, coarse, fine, jnp.zeros((seq_count, pad), jnp.bfloat16)], axis=1
    )

    def gather(tokens, bits):
        other = swap_ep(tokens, bits)
        return jnp.concatenate([tokens, other], axis=0), other

    rest = len(stages) - 3
    for bits in stages[:rest]:
        tokens, other = gather(tokens, bits)
    up = bring(up_block, [gate, other])
    gate = both((0,), gate.reshape(width, size))
    tokens, other = gather(tokens, stages[rest])
    down_a = bring(down_a_block, [up, other] + arrays(gate))
    up = both((1,), up.reshape(width, size))
    tokens, other = gather(tokens, stages[rest + 1])
    down_b = bring(down_b_block, [down_a, other] + arrays(up))
    down_a = both(0, down_a)
    tokens, _ = gather(tokens, stages[rest + 2])

    hidden = run_hidden(tokens, gate + up, width, ff, experts)
    lower = stages[-2::-1]
    orders = (lower, lower[1:] + lower[:1])
    pieces = down_a + [(None, cut, None, down_b)]
    products = run_down(hidden, pieces, count, rows, width)
    kept = products[0::2]
    given = [swap_ep(give, 1) for give in products[1::2]]
    totals = [
        reduce_blocks(add_terms(terms, other), lower, order, seq_count)
        for terms, other, order in zip(kept, given, orders)
    ]
    terms = jnp.concatenate(totals, axis=1).astype(jnp.float32)
    if parts > 1:
        terms = lax.psum_scatter(terms, "tp", scatter_dimension=1, tiled=True)
        own = width // parts
        stream = lax.dynamic_slice_in_dim(stream, lax.axis_index("tp") * own, own, 1)
    return (stream + terms).astype(jnp.bfloat16)


def solution(mesh):
    return jax.shard_map(
        shards,
        mesh=mesh,
        in_specs=(
            P(("grp", "ep"), "tp", None),
            P(("grp", "ep"), "tp", None),
            P(("grp", "ep"), "tp", None),
            P(("grp", "ep"), "tp", None, None),
            P(("grp", "ep"), "tp", None, None),
            P(("grp", "ep")),
            P(("grp", "ep"), None),
            P("tp", None),
            P(),
            P(("grp", "ep"), None),
            P(("grp", "ep"), None),
            P(None, None, "ep", "tp"),
        ),
        out_specs=P(("grp", "ep"), "tp"),
        check_vma=False,
    )
```

```python
import functools

import jax
import jax.numpy as jnp
from jax import lax
from jax.experimental import pallas as pl
from jax.experimental.pallas import tpu as pltpu
from jax.sharding import PartitionSpec as P

LANES = 128
PLANE = 4


def attend(queries, new_keys, new_values, cache_keys, cache_values, cache_lengths):
    seq_count, q_heads, head_size = queries.shape
    kv_heads = cache_keys.shape[1]
    length = cache_keys.shape[2]
    groups = q_heads // kv_heads
    score_scale = head_size ** (-0.5)
    grouped = queries.reshape(seq_count, kv_heads, groups, head_size)
    scores = (
        jnp.einsum("skgd,skld->skgl", grouped, cache_keys, preferred_element_type=jnp.float32)
        * score_scale
    )
    own_score = (
        jnp.einsum("skgd,skd->skg", grouped, new_keys, preferred_element_type=jnp.float32)
        * score_scale
    )
    live_mask = (
        jnp.arange(length, dtype=jnp.int32)[None, None, None, :]
        < cache_lengths[:, None, None, None]
    )
    masked = jnp.where(live_mask, scores, -1e30)
    row_top = jnp.maximum(jnp.max(masked, axis=-1), own_score)
    cache_exp = jnp.where(live_mask, jnp.exp(masked - row_top[..., None]), 0.0)
    own_exp = jnp.exp(own_score - row_top)
    row_total = jnp.sum(cache_exp, axis=-1) + own_exp
    probs_cache = (cache_exp / row_total[..., None]).astype(jnp.bfloat16)
    probs_own = (own_exp / row_total).astype(jnp.bfloat16)
    context = jnp.einsum(
        "skgl,skld->skgd", probs_cache, cache_values, preferred_element_type=jnp.float32
    )
    context = (
        context
        + probs_own.astype(jnp.float32)[..., None] * new_values.astype(jnp.float32)[:, :, None, :]
    )
    return context.astype(jnp.bfloat16).reshape(seq_count, q_heads * head_size)


def swap_ep(x, bits):
    count = lax.axis_size("ep")
    return lax.ppermute(x, "ep", [(i, i ^ bits) for i in range(count)])


def swap_grp(x):
    return lax.ppermute(x, "grp", [(0, 1), (1, 0)])


def after(values, others):
    if not others:
        return values
    return lax.optimization_barrier((tuple(values), tuple(others)))[0]


def load_weights(places, piece_refs, weights, sems, grp):
    half = weights.shape[-1] // 2
    copies = []
    for number, (matrix, side) in enumerate(places):
        if side is None:
            lanes = pl.ds(0, 2 * half)
        else:
            lanes = pl.ds(pl.multiple_of((grp ^ side) * half, LANES), half)
        target = weights.at[matrix, :, :, lanes]
        copies.append(pltpu.make_async_copy(piece_refs[number], target, sems.at[number]))
    for copy in copies:
        copy.start()
    for copy in copies:
        copy.wait()


def hidden_kernel(places, experts, where_ref, first_ref, second_ref, *refs):
    piece_refs, (out_ref, x_ref, weights, sems) = refs[:-4], refs[-4:]
    me = where_ref[0]
    step = pl.program_id(0)

    @pl.when(step == 0)
    def load():
        load_weights(places, piece_refs, weights, sems, where_ref[1])

    @pl.when(step < pl.num_programs(0) // 2)
    def early():
        x_ref[...] = first_ref[...]

    @pl.when(step >= pl.num_programs(0) // 2)
    def late():
        x_ref[...] = second_ref[...]

    width = weights.shape[1] * weights.shape[2]
    extra = x_ref[:, width:].astype(jnp.float32)
    lane = lax.broadcasted_iota(jnp.int32, extra.shape, 1)
    picked = jnp.where((lane == me) | (lane == me + experts), extra, 0.0)
    coef = jnp.sum(picked, axis=1, keepdims=True)
    x = x_ref[:, :width]
    ff = weights.shape[-1]
    gate = jnp.dot(x, weights[0].reshape(width, ff), preferred_element_type=jnp.float32)
    up = jnp.dot(x, weights[1].reshape(width, ff), preferred_element_type=jnp.float32)
    out_ref[...] = (gate / (1.0 + jnp.exp(-gate)) * up * coef).astype(jnp.bfloat16)


def down_kernel(cut, split, where_ref, hidden_ref, *refs):
    out_refs, weights = refs[-5:-1], refs[-1]
    mine_ref, whole_ref = refs[0], refs[1]
    me, grp = where_ref[0], where_ref[1]
    step = pl.program_id(0)
    half = weights.shape[-1] // 2
    weights[:, cut:, :] = whole_ref[...]
    if split:
        own = pl.ds(pl.multiple_of(grp * half, LANES), half)
        other = pl.ds(pl.multiple_of((1 - grp) * half, LANES), half)
        far_ref, near_refs = refs[2], refs[3:-5]
        weights[:, :cut, own] = mine_ref[...]

        @pl.when(step == me // PLANE)
        def near():
            for bits, ref in enumerate(near_refs):
                weights[pl.ds((me ^ bits) % PLANE, 1), :cut, other] = ref[...]

        @pl.when(step != me // PLANE)
        def far():
            weights[:, :cut, other] = far_ref[...]
    else:
        weights[:, :cut, :] = mine_ref[...]
    matrix = weights[...]
    down = lax.dot_general(
        hidden_ref[...],
        matrix.reshape(-1, matrix.shape[-1]),
        (((1,), (1,)), ((), ())),
        preferred_element_type=jnp.float32,
    )
    down = down.astype(jnp.bfloat16)
    size = out_refs[0].shape[0]
    turn = pl.num_programs(0) // 2
    for column in range(2):

        @pl.when((step >= turn) == (column == 1))
        def store(column=column):
            out_refs[2 * column][...] = down[:size]
            out_refs[2 * column + 1][...] = down[size:]


def run_hidden(first, second, pieces, places, shape, experts):
    total, ext = first.shape[0] * 2, first.shape[1]
    tile = 256 if total % 512 == 0 else total // 2
    steps = total // tile
    ff = shape[-1]
    where = jnp.stack([lax.axis_index("ep"), lax.axis_index("grp")]).astype(jnp.int32)
    grid_spec = pltpu.PrefetchScalarGridSpec(
        num_scalar_prefetch=1,
        grid=(steps,),
        in_specs=[
            pl.BlockSpec((tile, ext), lambda i, w: (jnp.minimum(i, steps // 2 - 1), 0)),
            pl.BlockSpec((tile, ext), lambda i, w: (jnp.maximum(i - steps // 2, 0), 0)),
        ]
        + [pl.BlockSpec(memory_space=pl.ANY)] * len(pieces),
        out_specs=pl.BlockSpec((tile, ff), lambda i, w: (i, 0)),
        scratch_shapes=[
            pltpu.VMEM((tile, ext), jnp.bfloat16),
            pltpu.VMEM(shape, jnp.bfloat16),
            pltpu.SemaphoreType.DMA((len(places),)),
        ],
    )
    return pl.pallas_call(
        functools.partial(hidden_kernel, places, experts),
        grid_spec=grid_spec,
        out_shape=jax.ShapeDtypeStruct((total, ff), jnp.bfloat16),
        compiler_params=pltpu.CompilerParams(vmem_limit_bytes=56 * 1024 * 1024),
    )(where, first, second, *pieces)


def run_down(hidden, mine, whole, far, near, rows, width):
    total, ff = hidden.shape
    count, cut, size = mine.shape
    block = PLANE if far is not None else min(max(PLANE, PLANE * LANES // rows), count // 2)
    steps = count // block
    where = jnp.stack([lax.axis_index("ep"), lax.axis_index("grp")]).astype(jnp.int32)
    spec = (total // 2, block * rows)
    low = pl.BlockSpec(spec, lambda i, w: (0, jnp.minimum(i, steps // 2 - 1)))
    high = pl.BlockSpec(spec, lambda i, w: (0, jnp.maximum(i - steps // 2, 0)))
    in_specs = [
        pl.BlockSpec((total, ff), lambda i, w: (0, 0)),
        pl.BlockSpec((block, cut, size), lambda i, w: (i, 0, 0)),
        pl.BlockSpec((block, rows - cut, ff), lambda i, w: (i, 0, 0)),
    ]
    pieces = [mine, whole]
    if far is not None:
        in_specs.append(
            pl.BlockSpec(
                (block, cut, size), lambda i, w: (jnp.maximum((i ^ (w[0] // PLANE)) - 1, 0), 0, 0)
            )
        )
        in_specs += [pl.BlockSpec((1, cut, size), lambda i, w: (0, 0, 0))] * len(near)
        pieces += [far] + near
    grid_spec = pltpu.PrefetchScalarGridSpec(
        num_scalar_prefetch=1,
        grid=(steps,),
        in_specs=in_specs,
        out_specs=[low, low, high, high],
        scratch_shapes=[pltpu.VMEM((block, rows, ff), jnp.bfloat16)],
    )
    return pl.pallas_call(
        functools.partial(down_kernel, cut, far is not None),
        grid_spec=grid_spec,
        out_shape=[jax.ShapeDtypeStruct((total // 2, width // 2), jnp.bfloat16)] * 4,
        compiler_params=pltpu.CompilerParams(vmem_limit_bytes=56 * 1024 * 1024),
    )(where, hidden, *pieces)


def add_terms(mine, other):
    return (mine.astype(jnp.float32) + other.astype(jnp.float32)).astype(jnp.bfloat16)


def fold(terms, axis, bits):
    keep = lax.index_in_dim(terms, 0, axis, keepdims=False)
    give = lax.index_in_dim(terms, 1, axis, keepdims=False)
    return add_terms(keep, swap_ep(give, bits))


def reduce_blocks(terms, left, order, seq_count):
    left = list(left)
    terms = terms.reshape((2,) * len(left) + (seq_count, terms.shape[1]))
    for bits in order:
        axis = left.index(bits)
        left.pop(axis)
        terms = fold(terms, axis, bits)
    return terms


def shards(
    queries,
    new_keys,
    new_values,
    cache_keys,
    cache_values,
    cache_lengths,
    residual,
    out_weight,
    norm_gain,
    expert_ids,
    route_weights,
    learner_weights,
):
    seq_count, width = residual.shape
    experts, _, rows, ff = learner_weights.shape
    count = lax.axis_size("ep")
    parts = lax.axis_size("tp")
    me = lax.axis_index("ep")
    grp = lax.axis_index("grp")
    stages = [1 << b for b in range(count.bit_length() - 2, -1, -1)]
    split = ff % (2 * LANES) == 0 and lax.axis_size("grp") == 2
    split = split and count % (2 * PLANE) == 0 and PLANE * rows % LANES == 0
    half = ff // 2

    def cut_out(matrix, low, high, halved, start):
        start, size = (start, half) if halved else (0, ff)
        return lax.dynamic_slice(
            learner_weights, (0, matrix, low, start), (experts, 1, high - low, size)
        )[:, 0]

    def bring(block, deps):
        (block,) = after([block], deps)
        return lax.all_to_all(block, "ep", split_axis=0, concat_axis=0, tiled=True)

    def swapped(mine):
        if not split:
            return None
        planes = [
            lax.dynamic_slice_in_dim(mine, ((me // PLANE) ^ k) * PLANE, PLANE, 0)
            for k in range(1, count // PLANE)
        ]
        return swap_grp(jnp.concatenate(planes, axis=0))

    def beside(bits, deps):
        (start,) = after([(1 - grp) * half], deps)
        block = lax.dynamic_slice(learner_weights, (me ^ bits, 2, 0, start), (1, 1, cut, half))[0]
        return swap_ep(block, bits) if bits else block

    def arrays(*values):
        return [value for value in values if value is not None]

    cut = rows * 3 // 4 // 16 * 16
    size = half if split else ff
    gate_block = cut_out(0, 0, rows, split, grp * half)
    (start,) = after([grp * half], [gate_block])
    up_block = cut_out(1, 0, rows, split, start)
    down_a_block = cut_out(2, 0, cut, split, start)
    down_b_block = cut_out(2, cut, rows, False, start)
    gate = bring(gate_block, [])
    (gate,) = after([gate], [up_block, down_a_block, down_b_block])

    context = attend(queries, new_keys, new_values, cache_keys, cache_values, cache_lengths)
    attn = jnp.dot(context, out_weight, preferred_element_type=jnp.float32)
    if parts > 1:
        attn = lax.psum(attn, "tp")
    stream = residual.astype(jnp.float32) + attn
    mean_square = jnp.mean(stream * stream, axis=1, keepdims=True)
    normed = (stream * lax.rsqrt(mean_square + 1e-06) * norm_gain).astype(jnp.bfloat16)

    hit = expert_ids[:, :, None] == jnp.arange(experts, dtype=jnp.int32)[None, None, :]
    coefs = jnp.sum(jnp.where(hit, route_weights[:, :, None], 0.0), axis=1)
    coarse = coefs.astype(jnp.bfloat16)
    fine = (coefs - coarse.astype(jnp.float32)).astype(jnp.bfloat16)
    pad = -(2 * experts) % LANES
    tokens = jnp.concatenate(
        [normed, coarse, fine, jnp.zeros((seq_count, pad), jnp.bfloat16)], axis=1
    )

    def gather(tokens, bits):
        other = swap_ep(tokens, bits)
        return jnp.concatenate([tokens, other], axis=0), other

    rest = len(stages) - 3
    for bits in stages[:rest]:
        tokens, other = gather(tokens, bits)
    up = bring(up_block, [gate, other])
    gate_far = swap_grp(gate) if split else None
    tokens, other = gather(tokens, stages[rest])
    down_a = bring(down_a_block, [up, other] + arrays(gate_far))
    near = [beside(bits, [up]) for bits in range(PLANE)] if split else []
    up_far = swap_grp(up) if split else None
    tokens, other = gather(tokens, stages[rest + 1])
    down_b = bring(down_b_block, [down_a, other] + arrays(up_far))
    down_a_far = swapped(down_a)
    other = swap_ep(tokens, stages[rest + 2])

    pieces, places = [], []
    side = 0 if split else None
    for matrix, (mine, far) in enumerate(((gate, gate_far), (up, up_far))):
        places.append((matrix, side))
        pieces.append(mine)
        if split:
            places.append((matrix, 1))
            pieces.append(far)
    hidden = run_hidden(tokens, other, pieces, places, (2, count, rows, ff), experts)
    lower = stages[-2::-1]
    orders = (lower, lower[1:] + lower[:1])
    products = run_down(hidden, down_a, down_b, down_a_far, near, rows, width)
    kept = products[0::2]
    given = [swap_ep(give, 1) for give in products[1::2]]
    totals = [
        reduce_blocks(add_terms(terms, other), lower, order, seq_count)
        for terms, other, order in zip(kept, given, orders)
    ]
    terms = jnp.concatenate(totals, axis=1).astype(jnp.float32)
    if parts > 1:
        terms = lax.psum_scatter(terms, "tp", scatter_dimension=1, tiled=True)
        own = width // parts
        stream = lax.dynamic_slice_in_dim(stream, lax.axis_index("tp") * own, own, 1)
    return (stream + terms).astype(jnp.bfloat16)


def solution(mesh):
    return jax.shard_map(
        shards,
        mesh=mesh,
        in_specs=(
            P(("grp", "ep"), "tp", None),
            P(("grp", "ep"), "tp", None),
            P(("grp", "ep"), "tp", None),
            P(("grp", "ep"), "tp", None, None),
            P(("grp", "ep"), "tp", None, None),
            P(("grp", "ep")),
            P(("grp", "ep"), None),
            P("tp", None),
            P(),
            P(("grp", "ep"), None),
            P(("grp", "ep"), None),
            P(None, None, "ep", "tp"),
        ),
        out_specs=P(("grp", "ep"), "tp"),
        check_vma=False,
    )
```

```python
import functools

import jax
import jax.numpy as jnp
from jax import lax
from jax.experimental import pallas as pl
from jax.experimental.pallas import tpu as pltpu
from jax.sharding import PartitionSpec as P

LANES = 128
PLANE = 4


def attend(queries, new_keys, new_values, cache_keys, cache_values, cache_lengths):
    seq_count, q_heads, head_size = queries.shape
    kv_heads = cache_keys.shape[1]
    length = cache_keys.shape[2]
    groups = q_heads // kv_heads
    score_scale = head_size ** (-0.5)
    grouped = queries.reshape(seq_count, kv_heads, groups, head_size)
    scores = (
        jnp.einsum("skgd,skld->skgl", grouped, cache_keys, preferred_element_type=jnp.float32)
        * score_scale
    )
    own_score = (
        jnp.einsum("skgd,skd->skg", grouped, new_keys, preferred_element_type=jnp.float32)
        * score_scale
    )
    live_mask = (
        jnp.arange(length, dtype=jnp.int32)[None, None, None, :]
        < cache_lengths[:, None, None, None]
    )
    masked = jnp.where(live_mask, scores, -1e30)
    row_top = jnp.maximum(jnp.max(masked, axis=-1), own_score)
    cache_exp = jnp.where(live_mask, jnp.exp(masked - row_top[..., None]), 0.0)
    own_exp = jnp.exp(own_score - row_top)
    row_total = jnp.sum(cache_exp, axis=-1) + own_exp
    probs_cache = (cache_exp / row_total[..., None]).astype(jnp.bfloat16)
    probs_own = (own_exp / row_total).astype(jnp.bfloat16)
    context = jnp.einsum(
        "skgl,skld->skgd", probs_cache, cache_values, preferred_element_type=jnp.float32
    )
    context = (
        context
        + probs_own.astype(jnp.float32)[..., None] * new_values.astype(jnp.float32)[:, :, None, :]
    )
    return context.astype(jnp.bfloat16).reshape(seq_count, q_heads * head_size)


def swap_ep(x, bits):
    count = lax.axis_size("ep")
    return lax.ppermute(x, "ep", [(i, i ^ bits) for i in range(count)])


def swap_grp(x):
    return lax.ppermute(x, "grp", [(0, 1), (1, 0)])


def after(values, others):
    if not others:
        return values
    return lax.optimization_barrier((tuple(values), tuple(others)))[0]


def load_weights(places, piece_refs, weights, sems, me, grp):
    half = weights.shape[-1] // 2
    copies = []
    for index, (number, part, matrix, sources, side) in enumerate(places):
        if sources is None:
            span = pl.ds(0, weights.shape[1])
        elif sources < PLANE:
            span = pl.ds(me ^ sources, 1)
        else:
            span = pl.ds(((me // PLANE) ^ (sources // PLANE)) * PLANE, PLANE)
        if side is None:
            lanes = pl.ds(0, 2 * half)
        else:
            lanes = pl.ds(pl.multiple_of((grp ^ side) * half, LANES), half)
        piece = piece_refs[number]
        if part is not None:
            piece = piece.at[part]
        target = weights.at[matrix, span, :, lanes]
        copies.append(pltpu.make_async_copy(piece, target, sems.at[index]))
    for copy in copies:
        copy.start()
    for copy in copies:
        copy.wait()


def hidden_kernel(places, experts, where_ref, first_ref, second_ref, *refs):
    piece_refs, (out_ref, x_ref, weights, sems) = refs[:-4], refs[-4:]
    me = where_ref[0]
    step = pl.program_id(0)

    @pl.when(step == 0)
    def load():
        load_weights(places, piece_refs, weights, sems, me, where_ref[1])

    @pl.when(step < pl.num_programs(0) // 2)
    def early():
        x_ref[...] = first_ref[...]

    @pl.when(step >= pl.num_programs(0) // 2)
    def late():
        x_ref[...] = second_ref[...]

    width = weights.shape[1] * weights.shape[2]
    extra = x_ref[:, width:].astype(jnp.float32)
    lane = lax.broadcasted_iota(jnp.int32, extra.shape, 1)
    picked = jnp.where((lane == me) | (lane == me + experts), extra, 0.0)
    coef = jnp.sum(picked, axis=1, keepdims=True)
    x = x_ref[:, :width]
    ff = weights.shape[-1]
    gate = jnp.dot(x, weights[0].reshape(width, ff), preferred_element_type=jnp.float32)
    up = jnp.dot(x, weights[1].reshape(width, ff), preferred_element_type=jnp.float32)
    out_ref[...] = (gate / (1.0 + jnp.exp(-gate)) * up * coef).astype(jnp.bfloat16)


def down_kernel(cut, split, where_ref, hidden_ref, *refs):
    out_refs, weights = refs[-5:-1], refs[-1]
    mine_ref, whole_ref = refs[0], refs[1]
    me, grp = where_ref[0], where_ref[1]
    step = pl.program_id(0)
    half = weights.shape[-1] // 2
    weights[:, cut:, :] = whole_ref[...]
    if split:
        own = pl.ds(pl.multiple_of(grp * half, LANES), half)
        other = pl.ds(pl.multiple_of((1 - grp) * half, LANES), half)
        far_ref, near_refs = refs[2], refs[3:-5]
        weights[:, :cut, own] = mine_ref[...]

        @pl.when(step == me // PLANE)
        def near():
            for bits, ref in enumerate(near_refs):
                weights[pl.ds((me ^ bits) % PLANE, 1), :cut, other] = ref[:, :cut, :]

        @pl.when(step != me // PLANE)
        def far():
            weights[:, :cut, other] = far_ref[...]
    else:
        weights[:, :cut, :] = mine_ref[...]
    matrix = weights[...]
    down = lax.dot_general(
        hidden_ref[...],
        matrix.reshape(-1, matrix.shape[-1]),
        (((1,), (1,)), ((), ())),
        preferred_element_type=jnp.float32,
    )
    down = down.astype(jnp.bfloat16)
    size = out_refs[0].shape[0]
    turn = pl.num_programs(0) // 2
    for column in range(2):

        @pl.when((step >= turn) == (column == 1))
        def store(column=column):
            out_refs[2 * column][...] = down[:size]
            out_refs[2 * column + 1][...] = down[size:]


def run_hidden(first, second, pieces, places, shape, experts):
    total, ext = first.shape[0] * 2, first.shape[1]
    tile = 256 if total % 512 == 0 else total // 2
    steps = total // tile
    ff = shape[-1]
    where = jnp.stack([lax.axis_index("ep"), lax.axis_index("grp")]).astype(jnp.int32)
    grid_spec = pltpu.PrefetchScalarGridSpec(
        num_scalar_prefetch=1,
        grid=(steps,),
        in_specs=[
            pl.BlockSpec((tile, ext), lambda i, w: (jnp.minimum(i, steps // 2 - 1), 0)),
            pl.BlockSpec((tile, ext), lambda i, w: (jnp.maximum(i - steps // 2, 0), 0)),
        ]
        + [pl.BlockSpec(memory_space=pl.ANY)] * len(pieces),
        out_specs=pl.BlockSpec((tile, ff), lambda i, w: (i, 0)),
        scratch_shapes=[
            pltpu.VMEM((tile, ext), jnp.bfloat16),
            pltpu.VMEM(shape, jnp.bfloat16),
            pltpu.SemaphoreType.DMA((len(places),)),
        ],
    )
    return pl.pallas_call(
        functools.partial(hidden_kernel, places, experts),
        grid_spec=grid_spec,
        out_shape=jax.ShapeDtypeStruct((total, ff), jnp.bfloat16),
        compiler_params=pltpu.CompilerParams(vmem_limit_bytes=56 * 1024 * 1024),
    )(where, first, second, *pieces)


def run_down(hidden, mine, whole, far, near, rows, width):
    total, ff = hidden.shape
    count, cut, size = mine.shape
    block = PLANE if far is not None else min(max(PLANE, PLANE * LANES // rows), count // 2)
    steps = count // block
    where = jnp.stack([lax.axis_index("ep"), lax.axis_index("grp")]).astype(jnp.int32)
    spec = (total // 2, block * rows)
    low = pl.BlockSpec(spec, lambda i, w: (0, jnp.minimum(i, steps // 2 - 1)))
    high = pl.BlockSpec(spec, lambda i, w: (0, jnp.maximum(i - steps // 2, 0)))
    in_specs = [
        pl.BlockSpec((total, ff), lambda i, w: (0, 0)),
        pl.BlockSpec((block, cut, size), lambda i, w: (i, 0, 0)),
        pl.BlockSpec((block, rows - cut, ff), lambda i, w: (i, 0, 0)),
    ]
    pieces = [mine, whole]
    if far is not None:
        in_specs.append(
            pl.BlockSpec(
                (block, cut, size), lambda i, w: (jnp.maximum((i ^ (w[0] // PLANE)) - 1, 0), 0, 0)
            )
        )
        in_specs += [pl.BlockSpec((1, rows, size), lambda i, w: (1, 0, 0))] * len(near)
        pieces += [far] + near
    grid_spec = pltpu.PrefetchScalarGridSpec(
        num_scalar_prefetch=1,
        grid=(steps,),
        in_specs=in_specs,
        out_specs=[low, low, high, high],
        scratch_shapes=[pltpu.VMEM((block, rows, ff), jnp.bfloat16)],
    )
    return pl.pallas_call(
        functools.partial(down_kernel, cut, far is not None),
        grid_spec=grid_spec,
        out_shape=[jax.ShapeDtypeStruct((total // 2, width // 2), jnp.bfloat16)] * 4,
        compiler_params=pltpu.CompilerParams(vmem_limit_bytes=56 * 1024 * 1024),
    )(where, hidden, *pieces)


def add_terms(mine, other):
    return (mine.astype(jnp.float32) + other.astype(jnp.float32)).astype(jnp.bfloat16)


def fold(terms, axis, bits):
    keep = lax.index_in_dim(terms, 0, axis, keepdims=False)
    give = lax.index_in_dim(terms, 1, axis, keepdims=False)
    return add_terms(keep, swap_ep(give, bits))


def reduce_blocks(terms, left, order, seq_count):
    left = list(left)
    terms = terms.reshape((2,) * len(left) + (seq_count, terms.shape[1]))
    for bits in order:
        axis = left.index(bits)
        left.pop(axis)
        terms = fold(terms, axis, bits)
    return terms


def shards(
    queries,
    new_keys,
    new_values,
    cache_keys,
    cache_values,
    cache_lengths,
    residual,
    out_weight,
    norm_gain,
    expert_ids,
    route_weights,
    learner_weights,
):
    seq_count, width = residual.shape
    experts, _, rows, ff = learner_weights.shape
    count = lax.axis_size("ep")
    parts = lax.axis_size("tp")
    me = lax.axis_index("ep")
    grp = lax.axis_index("grp")
    stages = [1 << b for b in range(count.bit_length() - 2, -1, -1)]
    split = ff % (2 * LANES) == 0 and lax.axis_size("grp") == 2
    split = split and count % (2 * PLANE) == 0 and PLANE * rows % LANES == 0
    half = ff // 2

    def cut_out(matrix, low, high, halved, start):
        start, size = (start, half) if halved else (0, ff)
        return lax.dynamic_slice(
            learner_weights, (0, matrix, low, start), (experts, 1, high - low, size)
        )[:, 0]

    def bring(block, deps):
        (block,) = after([block], deps)
        return lax.all_to_all(block, "ep", split_axis=0, concat_axis=0, tiled=True)

    def swapped(mine):
        if not split:
            return None
        planes = [
            lax.dynamic_slice_in_dim(mine, ((me // PLANE) ^ k) * PLANE, PLANE, 0)
            for k in range(1, count // PLANE)
        ]
        return swap_grp(jnp.concatenate(planes, axis=0))

    def beside(bits, deps):
        (start,) = after([(1 - grp) * half], deps)
        block = lax.dynamic_slice(learner_weights, (me ^ bits, 1, 0, start), (1, 2, rows, half))[0]
        return swap_ep(block, bits) if bits else block

    def arrays(*values):
        return [value for value in values if value is not None]

    cut = rows * 3 // 4 // 16 * 16
    size = half if split else ff
    gate_block = cut_out(0, 0, rows, split, grp * half)
    (start,) = after([grp * half], [gate_block])
    up_block = cut_out(1, 0, rows, split, start)
    down_a_block = cut_out(2, 0, cut, split, start)
    down_b_block = cut_out(2, cut, rows, False, start)
    gate = bring(gate_block, [])
    (gate,) = after([gate], [up_block, down_a_block, down_b_block])

    context = attend(queries, new_keys, new_values, cache_keys, cache_values, cache_lengths)
    attn = jnp.dot(context, out_weight, preferred_element_type=jnp.float32)
    if parts > 1:
        attn = lax.psum(attn, "tp")
    stream = residual.astype(jnp.float32) + attn
    mean_square = jnp.mean(stream * stream, axis=1, keepdims=True)
    normed = (stream * lax.rsqrt(mean_square + 1e-06) * norm_gain).astype(jnp.bfloat16)

    hit = expert_ids[:, :, None] == jnp.arange(experts, dtype=jnp.int32)[None, None, :]
    coefs = jnp.sum(jnp.where(hit, route_weights[:, :, None], 0.0), axis=1)
    coarse = coefs.astype(jnp.bfloat16)
    fine = (coefs - coarse.astype(jnp.float32)).astype(jnp.bfloat16)
    pad = -(2 * experts) % LANES
    tokens = jnp.concatenate(
        [normed, coarse, fine, jnp.zeros((seq_count, pad), jnp.bfloat16)], axis=1
    )

    def gather(tokens, bits):
        other = swap_ep(tokens, bits)
        return jnp.concatenate([tokens, other], axis=0), other

    rest = len(stages) - 3
    for bits in stages[:rest]:
        tokens, other = gather(tokens, bits)
    near = [beside(bits, []) for bits in range(PLANE)] if split else []
    up = bring(up_block, [gate, other] + near)
    gate_far = swap_grp(gate) if split else None
    tokens, other = gather(tokens, stages[rest])
    down_a = bring(down_a_block, [up, other] + arrays(gate_far))
    up_far = swapped(up)
    tokens, other = gather(tokens, stages[rest + 1])
    down_b = bring(down_b_block, [down_a, other] + arrays(up_far))
    down_a_far = swapped(down_a)
    other = swap_ep(tokens, stages[rest + 2])

    pieces, places = [], []
    side = 0 if split else None
    for matrix, (mine, far) in enumerate(((gate, gate_far), (up, up_far))):
        places.append((len(pieces), None, matrix, None, side))
        pieces.append(mine)
        if split and matrix == 0:
            places.append((len(pieces), None, matrix, None, 1))
            pieces.append(far)
        elif split:
            for k in range(1, count // PLANE):
                part = pl.ds((k - 1) * PLANE, PLANE)
                places.append((len(pieces), part, matrix, k * PLANE, 1))
            pieces.append(far)
    for bits, block in enumerate(near):
        places.append((len(pieces), pl.ds(0, 1), 1, bits, 1))
        pieces.append(block)
    hidden = run_hidden(tokens, other, pieces, places, (2, count, rows, ff), experts)
    lower = stages[-2::-1]
    orders = (lower, lower[1:-1] + lower[:1] + lower[-1:])
    products = run_down(hidden, down_a, down_b, down_a_far, near, rows, width)
    kept = products[0::2]
    given = [swap_ep(give, 1) for give in products[1::2]]
    totals = [
        reduce_blocks(add_terms(terms, other), lower, order, seq_count)
        for terms, other, order in zip(kept, given, orders)
    ]
    terms = jnp.concatenate(totals, axis=1).astype(jnp.float32)
    if parts > 1:
        terms = lax.psum_scatter(terms, "tp", scatter_dimension=1, tiled=True)
        own = width // parts
        stream = lax.dynamic_slice_in_dim(stream, lax.axis_index("tp") * own, own, 1)
    return (stream + terms).astype(jnp.bfloat16)


def solution(mesh):
    return jax.shard_map(
        shards,
        mesh=mesh,
        in_specs=(
            P(("grp", "ep"), "tp", None),
            P(("grp", "ep"), "tp", None),
            P(("grp", "ep"), "tp", None),
            P(("grp", "ep"), "tp", None, None),
            P(("grp", "ep"), "tp", None, None),
            P(("grp", "ep")),
            P(("grp", "ep"), None),
            P("tp", None),
            P(),
            P(("grp", "ep"), None),
            P(("grp", "ep"), None),
            P(None, None, "ep", "tp"),
        ),
        out_specs=P(("grp", "ep"), "tp"),
        check_vma=False,
    )
```

```python
import functools

import jax
import jax.numpy as jnp
from jax import lax
from jax.experimental import pallas as pl
from jax.experimental.pallas import tpu as pltpu
from jax.sharding import PartitionSpec as P

LANES = 128
PLANE, NEAR = 4, 2


def attend(queries, new_keys, new_values, cache_keys, cache_values, cache_lengths):
    seq_count, q_heads, head_size = queries.shape
    kv_heads = cache_keys.shape[1]
    length = cache_keys.shape[2]
    groups = q_heads // kv_heads
    score_scale = head_size ** (-0.5)
    grouped = queries.reshape(seq_count, kv_heads, groups, head_size)
    scores = (
        jnp.einsum("skgd,skld->skgl", grouped, cache_keys, preferred_element_type=jnp.float32)
        * score_scale
    )
    own_score = (
        jnp.einsum("skgd,skd->skg", grouped, new_keys, preferred_element_type=jnp.float32)
        * score_scale
    )
    live_mask = (
        jnp.arange(length, dtype=jnp.int32)[None, None, None, :]
        < cache_lengths[:, None, None, None]
    )
    masked = jnp.where(live_mask, scores, -1e30)
    row_top = jnp.maximum(jnp.max(masked, axis=-1), own_score)
    cache_exp = jnp.where(live_mask, jnp.exp(masked - row_top[..., None]), 0.0)
    own_exp = jnp.exp(own_score - row_top)
    row_total = jnp.sum(cache_exp, axis=-1) + own_exp
    probs_cache = (cache_exp / row_total[..., None]).astype(jnp.bfloat16)
    probs_own = (own_exp / row_total).astype(jnp.bfloat16)
    context = jnp.einsum(
        "skgl,skld->skgd", probs_cache, cache_values, preferred_element_type=jnp.float32
    )
    context = (
        context
        + probs_own.astype(jnp.float32)[..., None] * new_values.astype(jnp.float32)[:, :, None, :]
    )
    return context.astype(jnp.bfloat16).reshape(seq_count, q_heads * head_size)


def swap_ep(x, bits):
    count = lax.axis_size("ep")
    return lax.ppermute(x, "ep", [(i, i ^ bits) for i in range(count)])


def swap_grp(x):
    return lax.ppermute(x, "grp", [(0, 1), (1, 0)])


def after(values, others):
    if not others:
        return values
    return lax.optimization_barrier((tuple(values), tuple(others)))[0]


def load_weights(places, piece_refs, weights, sems, me, grp):
    half = weights.shape[-1] // 2
    copies = []
    for index, (number, part, matrix, sources, side) in enumerate(places):
        if sources is None:
            span = pl.ds(0, weights.shape[1])
        elif sources < PLANE:
            span = pl.ds(me ^ sources, 1)
        else:
            span = pl.ds(((me // PLANE) ^ (sources // PLANE)) * PLANE, PLANE)
        if side is None:
            lanes = pl.ds(0, 2 * half)
        else:
            lanes = pl.ds(pl.multiple_of((grp ^ side) * half, LANES), half)
        piece = piece_refs[number]
        if part is not None:
            piece = piece.at[part]
        target = weights.at[matrix, span, :, lanes]
        copies.append(pltpu.make_async_copy(piece, target, sems.at[index]))
    for copy in copies:
        copy.start()
    for copy in copies:
        copy.wait()


def hidden_kernel(places, experts, where_ref, first_ref, second_ref, *refs):
    piece_refs, (out_ref, x_ref, weights, sems) = refs[:-4], refs[-4:]
    me = where_ref[0]
    step = pl.program_id(0)

    @pl.when(step == 0)
    def load():
        load_weights(places, piece_refs, weights, sems, me, where_ref[1])

    @pl.when(step < pl.num_programs(0) // 2)
    def early():
        x_ref[...] = first_ref[...]

    @pl.when(step >= pl.num_programs(0) // 2)
    def late():
        x_ref[...] = second_ref[...]

    width = weights.shape[1] * weights.shape[2]
    extra = x_ref[:, width:].astype(jnp.float32)
    lane = lax.broadcasted_iota(jnp.int32, extra.shape, 1)
    picked = jnp.where((lane == me) | (lane == me + experts), extra, 0.0)
    coef = jnp.sum(picked, axis=1, keepdims=True)
    x = x_ref[:, :width]
    ff = weights.shape[-1]
    gate = jnp.dot(x, weights[0].reshape(width, ff), preferred_element_type=jnp.float32)
    up = jnp.dot(x, weights[1].reshape(width, ff), preferred_element_type=jnp.float32)
    out_ref[...] = (gate / (1.0 + jnp.exp(-gate)) * up * coef).astype(jnp.bfloat16)


def down_kernel(cut, split, where_ref, hidden_ref, *refs):
    out_refs, weights = refs[-5:-1], refs[-1]
    mine_ref, whole_ref = refs[0], refs[1]
    me, grp = where_ref[0], where_ref[1]
    step = pl.program_id(0)
    half = weights.shape[-1] // 2
    weights[:, cut:, :] = whole_ref[...]
    if split:
        own = pl.ds(pl.multiple_of(grp * half, LANES), half)
        other = pl.ds(pl.multiple_of((1 - grp) * half, LANES), half)
        far_ref, near_refs = refs[2], refs[3:-5]
        weights[:, :cut, own] = mine_ref[...]

        flipped = step ^ (me // PLANE)
        for plane in range(NEAR):

            @pl.when(flipped == plane)
            def near(plane=plane):
                for bits in range(PLANE):
                    block = near_refs[plane * PLANE + bits][:, :cut, :]
                    weights[pl.ds((me ^ bits) % PLANE, 1), :cut, other] = block

        @pl.when(flipped >= NEAR)
        def far():
            weights[:, :cut, other] = far_ref[...]
    else:
        weights[:, :cut, :] = mine_ref[...]
    matrix = weights[...]
    down = lax.dot_general(
        hidden_ref[...],
        matrix.reshape(-1, matrix.shape[-1]),
        (((1,), (1,)), ((), ())),
        preferred_element_type=jnp.float32,
    )
    down = down.astype(jnp.bfloat16)
    size = out_refs[0].shape[0]
    turn = pl.num_programs(0) // 2
    for column in range(2):

        @pl.when((step >= turn) == (column == 1))
        def store(column=column):
            out_refs[2 * column][...] = down[:size]
            out_refs[2 * column + 1][...] = down[size:]


def run_hidden(first, second, pieces, places, shape, experts):
    total, ext = first.shape[0] * 2, first.shape[1]
    tile = 256 if total % 512 == 0 else total // 2
    steps = total // tile
    ff = shape[-1]
    where = jnp.stack([lax.axis_index("ep"), lax.axis_index("grp")]).astype(jnp.int32)
    grid_spec = pltpu.PrefetchScalarGridSpec(
        num_scalar_prefetch=1,
        grid=(steps,),
        in_specs=[
            pl.BlockSpec((tile, ext), lambda i, w: (jnp.minimum(i, steps // 2 - 1), 0)),
            pl.BlockSpec((tile, ext), lambda i, w: (jnp.maximum(i - steps // 2, 0), 0)),
        ]
        + [pl.BlockSpec(memory_space=pl.ANY)] * len(pieces),
        out_specs=pl.BlockSpec((tile, ff), lambda i, w: (i, 0)),
        scratch_shapes=[
            pltpu.VMEM((tile, ext), jnp.bfloat16),
            pltpu.VMEM(shape, jnp.bfloat16),
            pltpu.SemaphoreType.DMA((len(places),)),
        ],
    )
    return pl.pallas_call(
        functools.partial(hidden_kernel, places, experts),
        grid_spec=grid_spec,
        out_shape=jax.ShapeDtypeStruct((total, ff), jnp.bfloat16),
        compiler_params=pltpu.CompilerParams(vmem_limit_bytes=56 * 1024 * 1024),
    )(where, first, second, *pieces)


def run_down(hidden, mine, whole, far, near, rows, width):
    total, ff = hidden.shape
    count, cut, size = mine.shape
    block = PLANE if far is not None else min(max(PLANE, PLANE * LANES // rows), count // 2)
    steps = count // block
    where = jnp.stack([lax.axis_index("ep"), lax.axis_index("grp")]).astype(jnp.int32)
    spec = (total // 2, block * rows)
    low = pl.BlockSpec(spec, lambda i, w: (0, jnp.minimum(i, steps // 2 - 1)))
    high = pl.BlockSpec(spec, lambda i, w: (0, jnp.maximum(i - steps // 2, 0)))
    in_specs = [
        pl.BlockSpec((total, ff), lambda i, w: (0, 0)),
        pl.BlockSpec((block, cut, size), lambda i, w: (i, 0, 0)),
        pl.BlockSpec((block, rows - cut, ff), lambda i, w: (i, 0, 0)),
    ]
    pieces = [mine, whole]
    if far is not None:

        def from_far(i, w):
            return jnp.maximum((i ^ (w[0] // PLANE)) - NEAR, 0), 0, 0

        in_specs.append(pl.BlockSpec((block, cut, size), from_far))
        for array in near:
            last, height = array.shape[0] - 1, array.shape[1]
            in_specs.append(pl.BlockSpec((1, height, size), lambda i, w, last=last: (last, 0, 0)))
        pieces += [far] + near
    grid_spec = pltpu.PrefetchScalarGridSpec(
        num_scalar_prefetch=1,
        grid=(steps,),
        in_specs=in_specs,
        out_specs=[low, low, high, high],
        scratch_shapes=[pltpu.VMEM((block, rows, ff), jnp.bfloat16)],
    )
    return pl.pallas_call(
        functools.partial(down_kernel, cut, far is not None),
        grid_spec=grid_spec,
        out_shape=[jax.ShapeDtypeStruct((total // 2, width // 2), jnp.bfloat16)] * 4,
        compiler_params=pltpu.CompilerParams(vmem_limit_bytes=56 * 1024 * 1024),
    )(where, hidden, *pieces)


def add_terms(mine, other):
    return (mine.astype(jnp.float32) + other.astype(jnp.float32)).astype(jnp.bfloat16)


def fold(terms, axis, bits):
    keep = lax.index_in_dim(terms, 0, axis, keepdims=False)
    give = lax.index_in_dim(terms, 1, axis, keepdims=False)
    return add_terms(keep, swap_ep(give, bits))


def reduce_blocks(terms, left, order, seq_count):
    left = list(left)
    terms = terms.reshape((2,) * len(left) + (seq_count, terms.shape[1]))
    for bits in order:
        axis = left.index(bits)
        left.pop(axis)
        terms = fold(terms, axis, bits)
    return terms


def shards(
    queries,
    new_keys,
    new_values,
    cache_keys,
    cache_values,
    cache_lengths,
    residual,
    out_weight,
    norm_gain,
    expert_ids,
    route_weights,
    learner_weights,
):
    seq_count, width = residual.shape
    experts, _, rows, ff = learner_weights.shape
    count = lax.axis_size("ep")
    parts = lax.axis_size("tp")
    me = lax.axis_index("ep")
    grp = lax.axis_index("grp")
    stages = [1 << b for b in range(count.bit_length() - 2, -1, -1)]
    split = ff % (2 * LANES) == 0 and lax.axis_size("grp") == 2
    split = split and count >= 2 * NEAR * PLANE and PLANE * rows % LANES == 0
    half = ff // 2

    def cut_out(matrix, low, high, halved, start):
        start, size = (start, half) if halved else (0, ff)
        return lax.dynamic_slice(
            learner_weights, (0, matrix, low, start), (experts, 1, high - low, size)
        )[:, 0]

    def bring(block, deps):
        (block,) = after([block], deps)
        return lax.all_to_all(block, "ep", split_axis=0, concat_axis=0, tiled=True)

    def swapped(mine, first):
        if not split:
            return None
        planes = [
            lax.dynamic_slice_in_dim(mine, ((me // PLANE) ^ k) * PLANE, PLANE, 0)
            for k in range(first, count // PLANE)
        ]
        return swap_grp(jnp.concatenate(planes, axis=0))

    def beside(bits, deps):
        (start,) = after([(1 - grp) * half], deps)
        first, height = (1, rows) if bits < PLANE else (2, cut)
        block = lax.dynamic_slice(
            learner_weights, (me ^ bits, first, 0, start), (1, 3 - first, height, half)
        )[0]
        return swap_ep(block, bits) if bits else block

    def arrays(*values):
        return [value for value in values if value is not None]

    cut = rows * 3 // 4 // 16 * 16
    size = half if split else ff
    gate_block = cut_out(0, 0, rows, split, grp * half)
    (start,) = after([grp * half], [gate_block])
    up_block = cut_out(1, 0, rows, split, start)
    down_a_block = cut_out(2, 0, cut, split, start)
    down_b_block = cut_out(2, cut, rows, False, start)
    gate = bring(gate_block, [])
    (gate,) = after([gate], [up_block, down_a_block, down_b_block])

    context = attend(queries, new_keys, new_values, cache_keys, cache_values, cache_lengths)
    attn = jnp.dot(context, out_weight, preferred_element_type=jnp.float32)
    if parts > 1:
        attn = lax.psum(attn, "tp")
    stream = residual.astype(jnp.float32) + attn
    mean_square = jnp.mean(stream * stream, axis=1, keepdims=True)
    normed = (stream * lax.rsqrt(mean_square + 1e-06) * norm_gain).astype(jnp.bfloat16)

    hit = expert_ids[:, :, None] == jnp.arange(experts, dtype=jnp.int32)[None, None, :]
    coefs = jnp.sum(jnp.where(hit, route_weights[:, :, None], 0.0), axis=1)
    coarse = coefs.astype(jnp.bfloat16)
    fine = (coefs - coarse.astype(jnp.float32)).astype(jnp.bfloat16)
    pad = -(2 * experts) % LANES
    tokens = jnp.concatenate(
        [normed, coarse, fine, jnp.zeros((seq_count, pad), jnp.bfloat16)], axis=1
    )

    def gather(tokens, bits):
        other = swap_ep(tokens, bits)
        return jnp.concatenate([tokens, other], axis=0), other

    rest = len(stages) - 3
    for bits in stages[:rest]:
        tokens, other = gather(tokens, bits)
    near = [beside(bits, []) for bits in range(PLANE)] if split else []
    up = bring(up_block, [gate, other] + near)
    gate_far = swap_grp(gate) if split else None
    if split:
        near += [beside(bits, [gate]) for bits in range(PLANE, NEAR * PLANE)]
    tokens, other = gather(tokens, stages[rest])
    down_a = bring(down_a_block, [up, other] + arrays(gate_far) + near[PLANE:])
    up_far = swapped(up, 1)
    tokens, other = gather(tokens, stages[rest + 1])
    down_b = bring(down_b_block, [down_a, other] + arrays(up_far))
    down_a_far = swapped(down_a, NEAR)
    other = swap_ep(tokens, stages[rest + 2])

    pieces, places = [], []
    side = 0 if split else None
    for matrix, (mine, far) in enumerate(((gate, gate_far), (up, up_far))):
        places.append((len(pieces), None, matrix, None, side))
        pieces.append(mine)
        if split and matrix == 0:
            places.append((len(pieces), None, matrix, None, 1))
            pieces.append(far)
        elif split:
            for k in range(1, count // PLANE):
                part = pl.ds((k - 1) * PLANE, PLANE)
                places.append((len(pieces), part, matrix, k * PLANE, 1))
            pieces.append(far)
    for bits, block in enumerate(near[:PLANE]):
        places.append((len(pieces), pl.ds(0, 1), 1, bits, 1))
        pieces.append(block)
    hidden = run_hidden(tokens, other, pieces, places, (2, count, rows, ff), experts)
    lower = stages[-2::-1]
    orders = (lower, lower[1:-1] + lower[:1] + lower[-1:])
    products = run_down(hidden, down_a, down_b, down_a_far, near, rows, width)
    kept = products[0::2]
    given = [swap_ep(give, 1) for give in products[1::2]]
    totals = [
        reduce_blocks(add_terms(terms, other), lower, order, seq_count)
        for terms, other, order in zip(kept, given, orders)
    ]
    terms = jnp.concatenate(totals, axis=1).astype(jnp.float32)
    if parts > 1:
        terms = lax.psum_scatter(terms, "tp", scatter_dimension=1, tiled=True)
        own = width // parts
        stream = lax.dynamic_slice_in_dim(stream, lax.axis_index("tp") * own, own, 1)
    return (stream + terms).astype(jnp.bfloat16)


def solution(mesh):
    return jax.shard_map(
        shards,
        mesh=mesh,
        in_specs=(
            P(("grp", "ep"), "tp", None),
            P(("grp", "ep"), "tp", None),
            P(("grp", "ep"), "tp", None),
            P(("grp", "ep"), "tp", None, None),
            P(("grp", "ep"), "tp", None, None),
            P(("grp", "ep")),
            P(("grp", "ep"), None),
            P("tp", None),
            P(),
            P(("grp", "ep"), None),
            P(("grp", "ep"), None),
            P(None, None, "ep", "tp"),
        ),
        out_specs=P(("grp", "ep"), "tp"),
        check_vma=False,
    )
```

```python
import functools

import jax
import jax.numpy as jnp
from jax import lax
from jax.experimental import pallas as pl
from jax.experimental.pallas import tpu as pltpu
from jax.sharding import PartitionSpec as P

LANES = 128
PLANE, NEAR = 4, 2


def attend(queries, new_keys, new_values, cache_keys, cache_values, cache_lengths):
    seq_count, q_heads, head_size = queries.shape
    kv_heads = cache_keys.shape[1]
    length = cache_keys.shape[2]
    groups = q_heads // kv_heads
    score_scale = head_size ** (-0.5)
    grouped = queries.reshape(seq_count, kv_heads, groups, head_size)
    scores = (
        jnp.einsum("skgd,skld->skgl", grouped, cache_keys, preferred_element_type=jnp.float32)
        * score_scale
    )
    own_score = (
        jnp.einsum("skgd,skd->skg", grouped, new_keys, preferred_element_type=jnp.float32)
        * score_scale
    )
    live_mask = (
        jnp.arange(length, dtype=jnp.int32)[None, None, None, :]
        < cache_lengths[:, None, None, None]
    )
    masked = jnp.where(live_mask, scores, -1e30)
    row_top = jnp.maximum(jnp.max(masked, axis=-1), own_score)
    cache_exp = jnp.where(live_mask, jnp.exp(masked - row_top[..., None]), 0.0)
    own_exp = jnp.exp(own_score - row_top)
    row_total = jnp.sum(cache_exp, axis=-1) + own_exp
    probs_cache = (cache_exp / row_total[..., None]).astype(jnp.bfloat16)
    probs_own = (own_exp / row_total).astype(jnp.bfloat16)
    context = jnp.einsum(
        "skgl,skld->skgd", probs_cache, cache_values, preferred_element_type=jnp.float32
    )
    context = (
        context
        + probs_own.astype(jnp.float32)[..., None] * new_values.astype(jnp.float32)[:, :, None, :]
    )
    return context.astype(jnp.bfloat16).reshape(seq_count, q_heads * head_size)


def swap_ep(x, bits):
    count = lax.axis_size("ep")
    return lax.ppermute(x, "ep", [(i, i ^ bits) for i in range(count)])


def swap_grp(x):
    return lax.ppermute(x, "grp", [(0, 1), (1, 0)])


def after(values, others):
    if not others:
        return values
    return lax.optimization_barrier((tuple(values), tuple(others)))[0]


def load_weights(places, piece_refs, weights, sems, me, grp):
    half = weights.shape[-1] // 2
    copies = []
    for index, (number, part, matrix, sources, side) in enumerate(places):
        if sources is None:
            span = pl.ds(0, weights.shape[1])
        elif sources < PLANE:
            span = pl.ds(me ^ sources, 1)
        else:
            span = pl.ds(((me // PLANE) ^ (sources // PLANE)) * PLANE, PLANE)
        if side is None:
            lanes = pl.ds(0, 2 * half)
        else:
            lanes = pl.ds(pl.multiple_of((grp ^ side) * half, LANES), half)
        piece = piece_refs[number]
        if part is not None:
            piece = piece.at[part]
        target = weights.at[matrix, span, :, lanes]
        copies.append(pltpu.make_async_copy(piece, target, sems.at[index]))
    for copy in copies:
        copy.start()
    for copy in copies:
        copy.wait()


def hidden_kernel(places, experts, where_ref, first_ref, second_ref, *refs):
    piece_refs, (out_ref, x_ref, weights, sems) = refs[:-4], refs[-4:]
    me = where_ref[0]
    step = pl.program_id(0)

    @pl.when(step == 0)
    def load():
        load_weights(places, piece_refs, weights, sems, me, where_ref[1])

    @pl.when(step < pl.num_programs(0) // 2)
    def early():
        x_ref[...] = first_ref[...]

    @pl.when(step >= pl.num_programs(0) // 2)
    def late():
        x_ref[...] = second_ref[...]

    width = weights.shape[1] * weights.shape[2]
    extra = x_ref[:, width:].astype(jnp.float32)
    lane = lax.broadcasted_iota(jnp.int32, extra.shape, 1)
    picked = jnp.where((lane == me) | (lane == me + experts), extra, 0.0)
    coef = jnp.sum(picked, axis=1, keepdims=True)
    x = x_ref[:, :width]
    ff = weights.shape[-1]
    gate = jnp.dot(x, weights[0].reshape(width, ff), preferred_element_type=jnp.float32)
    up = jnp.dot(x, weights[1].reshape(width, ff), preferred_element_type=jnp.float32)
    out_ref[...] = (gate / (1.0 + jnp.exp(-gate)) * up * coef).astype(jnp.bfloat16)


def down_kernel(cut, split, where_ref, hidden_ref, *refs):
    out_refs, weights = refs[-5:-1], refs[-1]
    mine_ref, whole_ref = refs[0], refs[1]
    me, grp = where_ref[0], where_ref[1]
    step = pl.program_id(0)
    half = weights.shape[-1] // 2
    weights[:, cut:, :] = whole_ref[...]
    if split:
        own = pl.ds(pl.multiple_of(grp * half, LANES), half)
        other = pl.ds(pl.multiple_of((1 - grp) * half, LANES), half)
        far_ref, near_refs = refs[2], refs[3:-5]
        weights[:, :cut, own] = mine_ref[...]

        flipped = step ^ (me // PLANE)
        for plane in range(NEAR):

            @pl.when(flipped == plane)
            def near(plane=plane):
                for bits in range(PLANE):
                    block = near_refs[plane * PLANE + bits][:, :cut, :]
                    weights[pl.ds((me ^ bits) % PLANE, 1), :cut, other] = block

        @pl.when(flipped >= NEAR)
        def far():
            weights[:, :cut, other] = far_ref[...]
    else:
        weights[:, :cut, :] = mine_ref[...]
    matrix = weights[...]
    down = lax.dot_general(
        hidden_ref[...],
        matrix.reshape(-1, matrix.shape[-1]),
        (((1,), (1,)), ((), ())),
        preferred_element_type=jnp.float32,
    )
    down = down.astype(jnp.bfloat16)
    size = out_refs[0].shape[0]
    turn = pl.num_programs(0) // 2
    for column in range(2):

        @pl.when((step >= turn) == (column == 1))
        def store(column=column):
            out_refs[2 * column][...] = down[:size]
            out_refs[2 * column + 1][...] = down[size:]


def run_hidden(first, second, pieces, places, shape, experts):
    total, ext = first.shape[0] * 2, first.shape[1]
    tile = 256 if total % 512 == 0 else total // 2
    steps = total // tile
    ff = shape[-1]
    where = jnp.stack([lax.axis_index("ep"), lax.axis_index("grp")]).astype(jnp.int32)
    grid_spec = pltpu.PrefetchScalarGridSpec(
        num_scalar_prefetch=1,
        grid=(steps,),
        in_specs=[
            pl.BlockSpec((tile, ext), lambda i, w: (jnp.minimum(i, steps // 2 - 1), 0)),
            pl.BlockSpec((tile, ext), lambda i, w: (jnp.maximum(i - steps // 2, 0), 0)),
        ]
        + [pl.BlockSpec(memory_space=pl.ANY)] * len(pieces),
        out_specs=pl.BlockSpec((tile, ff), lambda i, w: (i, 0)),
        scratch_shapes=[
            pltpu.VMEM((tile, ext), jnp.bfloat16),
            pltpu.VMEM(shape, jnp.bfloat16),
            pltpu.SemaphoreType.DMA((len(places),)),
        ],
    )
    return pl.pallas_call(
        functools.partial(hidden_kernel, places, experts),
        grid_spec=grid_spec,
        out_shape=jax.ShapeDtypeStruct((total, ff), jnp.bfloat16),
        compiler_params=pltpu.CompilerParams(vmem_limit_bytes=56 * 1024 * 1024),
    )(where, first, second, *pieces)


def run_down(hidden, mine, whole, far, near, rows, width):
    total, ff = hidden.shape
    count, cut, size = mine.shape
    block = PLANE if far is not None else min(max(PLANE, PLANE * LANES // rows), count // 2)
    steps = count // block
    where = jnp.stack([lax.axis_index("ep"), lax.axis_index("grp")]).astype(jnp.int32)
    spec = (total // 2, block * rows)
    low = pl.BlockSpec(spec, lambda i, w: (0, jnp.minimum(i, steps // 2 - 1)))
    high = pl.BlockSpec(spec, lambda i, w: (0, jnp.maximum(i - steps // 2, 0)))
    in_specs = [
        pl.BlockSpec((total, ff), lambda i, w: (0, 0)),
        pl.BlockSpec((block, cut, size), lambda i, w: (i, 0, 0)),
        pl.BlockSpec((block, rows - cut, ff), lambda i, w: (i, 0, 0)),
    ]
    pieces = [mine, whole]
    if far is not None:

        def from_far(i, w):
            return jnp.maximum((i ^ (w[0] // PLANE)) - NEAR, 0), 0, 0

        in_specs.append(pl.BlockSpec((block, cut, size), from_far))
        for array in near:
            last, height = array.shape[0] - 1, array.shape[1]
            in_specs.append(pl.BlockSpec((1, height, size), lambda i, w, last=last: (last, 0, 0)))
        pieces += [far] + near
    grid_spec = pltpu.PrefetchScalarGridSpec(
        num_scalar_prefetch=1,
        grid=(steps,),
        in_specs=in_specs,
        out_specs=[low, low, high, high],
        scratch_shapes=[pltpu.VMEM((block, rows, ff), jnp.bfloat16)],
    )
    return pl.pallas_call(
        functools.partial(down_kernel, cut, far is not None),
        grid_spec=grid_spec,
        out_shape=[jax.ShapeDtypeStruct((total // 2, width // 2), jnp.bfloat16)] * 4,
        compiler_params=pltpu.CompilerParams(vmem_limit_bytes=56 * 1024 * 1024),
    )(where, hidden, *pieces)


def add_terms(mine, other):
    return (mine.astype(jnp.float32) + other.astype(jnp.float32)).astype(jnp.bfloat16)


def fold(terms, axis, bits):
    keep = lax.index_in_dim(terms, 0, axis, keepdims=False)
    give = lax.index_in_dim(terms, 1, axis, keepdims=False)
    return add_terms(keep, swap_ep(give, bits))


def reduce_blocks(terms, left, order, seq_count):
    left = list(left)
    terms = terms.reshape((2,) * len(left) + (seq_count, terms.shape[1]))
    for bits in order:
        axis = left.index(bits)
        left.pop(axis)
        terms = fold(terms, axis, bits)
    return terms


def shards(
    queries,
    new_keys,
    new_values,
    cache_keys,
    cache_values,
    cache_lengths,
    residual,
    out_weight,
    norm_gain,
    expert_ids,
    route_weights,
    learner_weights,
):
    seq_count, width = residual.shape
    experts, _, rows, ff = learner_weights.shape
    count = lax.axis_size("ep")
    parts = lax.axis_size("tp")
    me = lax.axis_index("ep")
    grp = lax.axis_index("grp")
    stages = [1 << b for b in range(count.bit_length() - 2, -1, -1)]
    split = ff % (2 * LANES) == 0 and lax.axis_size("grp") == 2
    split = split and count >= 2 * NEAR * PLANE and PLANE * rows % LANES == 0
    half = ff // 2

    def cut_out(matrix, low, high, halved, start):
        start, size = (start, half) if halved else (0, ff)
        return lax.dynamic_slice(
            learner_weights, (0, matrix, low, start), (experts, 1, high - low, size)
        )[:, 0]

    def bring(block, deps):
        (block,) = after([block], deps)
        return lax.all_to_all(block, "ep", split_axis=0, concat_axis=0, tiled=True)

    def swapped(mine, first):
        if not split:
            return None
        planes = [
            lax.dynamic_slice_in_dim(mine, ((me // PLANE) ^ k) * PLANE, PLANE, 0)
            for k in range(first, count // PLANE)
        ]
        return swap_grp(jnp.concatenate(planes, axis=0))

    def beside(bits, deps):
        (start,) = after([(1 - grp) * half], deps)
        first, height = (1, rows) if bits < PLANE else (2, cut)
        block = lax.dynamic_slice(
            learner_weights, (me ^ bits, first, 0, start), (1, 3 - first, height, half)
        )[0]
        return swap_ep(block, bits) if bits else block

    def arrays(*values):
        return [value for value in values if value is not None]

    cut = rows * 3 // 4 // 16 * 16
    size = half if split else ff
    gate_block = cut_out(0, 0, rows, split, grp * half)
    (start,) = after([grp * half], [gate_block])
    up_block = cut_out(1, 0, rows, split, start)
    down_a_block = cut_out(2, 0, cut, split, start)
    down_b_block = cut_out(2, cut, rows, False, start)
    gate = bring(gate_block, [])
    (gate,) = after([gate], [up_block, down_a_block, down_b_block])

    context = attend(queries, new_keys, new_values, cache_keys, cache_values, cache_lengths)
    attn = jnp.dot(context, out_weight, preferred_element_type=jnp.float32)
    if parts > 1:
        attn = lax.psum(attn, "tp")
    stream = residual.astype(jnp.float32) + attn
    mean_square = jnp.mean(stream * stream, axis=1, keepdims=True)
    normed = (stream * lax.rsqrt(mean_square + 1e-06) * norm_gain).astype(jnp.bfloat16)

    hit = expert_ids[:, :, None] == jnp.arange(experts, dtype=jnp.int32)[None, None, :]
    coefs = jnp.sum(jnp.where(hit, route_weights[:, :, None], 0.0), axis=1)
    coarse = coefs.astype(jnp.bfloat16)
    fine = (coefs - coarse.astype(jnp.float32)).astype(jnp.bfloat16)
    pad = -(2 * experts) % LANES
    tokens = jnp.concatenate(
        [normed, coarse, fine, jnp.zeros((seq_count, pad), jnp.bfloat16)], axis=1
    )

    def gather(tokens, bits):
        other = swap_ep(tokens, bits)
        return jnp.concatenate([tokens, other], axis=0), other

    rest = len(stages) - 3
    for bits in stages[:rest]:
        tokens, other = gather(tokens, bits)
    near = [beside(bits, []) for bits in range(PLANE)] if split else []
    up = bring(up_block, [gate, other] + near)
    gate_far = swap_grp(gate) if split else None
    if split:
        near += [beside(bits, [gate]) for bits in range(PLANE, NEAR * PLANE)]
    tokens, other = gather(tokens, stages[rest])
    down_a = bring(down_a_block, [up, other] + arrays(gate_far) + near[PLANE:-2])
    up_far = swapped(up, 1)
    tokens, other = gather(tokens, stages[rest + 1])
    down_b = bring(down_b_block, [down_a, other] + arrays(up_far))
    down_a_far = swapped(down_a, NEAR)
    other = swap_ep(tokens, stages[rest + 2])

    pieces, places = [], []
    side = 0 if split else None
    for matrix, (mine, far) in enumerate(((gate, gate_far), (up, up_far))):
        places.append((len(pieces), None, matrix, None, side))
        pieces.append(mine)
        if split and matrix == 0:
            places.append((len(pieces), None, matrix, None, 1))
            pieces.append(far)
        elif split:
            for k in range(1, count // PLANE):
                part = pl.ds((k - 1) * PLANE, PLANE)
                places.append((len(pieces), part, matrix, k * PLANE, 1))
            pieces.append(far)
    for bits, block in enumerate(near[:PLANE]):
        places.append((len(pieces), pl.ds(0, 1), 1, bits, 1))
        pieces.append(block)
    hidden = run_hidden(tokens, other, pieces, places, (2, count, rows, ff), experts)
    lower = stages[-2::-1]
    orders = (lower, lower[1:-1] + lower[:1] + lower[-1:])
    products = run_down(hidden, down_a, down_b, down_a_far, near, rows, width)
    kept = products[0::2]
    given = [swap_ep(give, 1) for give in products[1::2]]
    totals = [
        reduce_blocks(add_terms(terms, other), lower, order, seq_count)
        for terms, other, order in zip(kept, given, orders)
    ]
    terms = jnp.concatenate(totals, axis=1).astype(jnp.float32)
    if parts > 1:
        terms = lax.psum_scatter(terms, "tp", scatter_dimension=1, tiled=True)
        own = width // parts
        stream = lax.dynamic_slice_in_dim(stream, lax.axis_index("tp") * own, own, 1)
    return (stream + terms).astype(jnp.bfloat16)


def solution(mesh):
    return jax.shard_map(
        shards,
        mesh=mesh,
        in_specs=(
            P(("grp", "ep"), "tp", None),
            P(("grp", "ep"), "tp", None),
            P(("grp", "ep"), "tp", None),
            P(("grp", "ep"), "tp", None, None),
            P(("grp", "ep"), "tp", None, None),
            P(("grp", "ep")),
            P(("grp", "ep"), None),
            P("tp", None),
            P(),
            P(("grp", "ep"), None),
            P(("grp", "ep"), None),
            P(None, None, "ep", "tp"),
        ),
        out_specs=P(("grp", "ep"), "tp"),
        check_vma=False,
    )
```
